32 devices in a mesh: dp: 2 (over y), cls: 16 (over z, x, core).
Axes of the slice: x: 2, y: 2, z: 4, core: 2. Of those that a mesh axis runs over, the one named last changes fastest.
Arguments:
- embeddings: bfloat16 [1152, 4096], P('dp'), may hold values from -128 to 128
- fold_ids: int32 [1152], P('dp'), may hold values from 0 to 4
- labels: int32 [1152], P('dp'), may hold values from 0 to 1023
- weights: bfloat16 [4096, 5120], P('dp', 'cls'), may hold values from -4 to 4
- direction: bfloat16 [4096, 5120], P('dp', 'cls'), may hold values from -0.09375 to 0.09375
Outputs:
- gradient: float32 [4096, 5120], P('dp', 'cls')
- hess_vec: float32 [4096, 5120], P('dp', 'cls')
The draws below stay inside these ranges and needn't reach their ends.
All inputs are finite; a program needn't handle non-finite values.
Results may differ from the reference program's by a relative error of at most 0.0055.
Values may be sent and summed in bfloat16 or wider, within the bound.
A program may use at most 64 MiB of HBM per device.

```python
import math
import jax
import jax.numpy as jnp
from jax import lax

D = 4096
CLASSES = 1024
FOLDS = 5
ROWS = 1152
COLS = 5120


def weight_table(key):
    noise = jax.random.normal(jax.random.fold_in(key, 11), (D, COLS), jnp.float32)
    table = jnp.clip(noise, -6.0, 6.0) * (3.0 / math.sqrt(D))
    return table


def draw_weights(key, part):
    return weight_table(key).astype(jnp.bfloat16)


def draw_embeddings(key, part):
    base = jnp.clip(jax.random.normal(jax.random.fold_in(key, 23), (ROWS, D), jnp.float32), -6.0, 6.0)
    spread = jax.random.uniform(jax.random.fold_in(key, 24), (ROWS, 1), jnp.float32, math.log(0.4), math.log(4.0))
    values = base * jnp.exp(spread)
    return jnp.clip(values, -128.0, 128.0).astype(jnp.bfloat16)


def place_ends(values, own_key, low, high):
    longest = values.shape.index(max(values.shape))
    spots = []
    for shift in (0, 1):
        where = [jax.random.randint(jax.random.fold_in(own_key, axis), (), 0, length) for axis, length in enumerate(values.shape)]
        where[longest] = (where[longest] + shift) % values.shape[longest]
        spots.append(tuple(where))
    return values.at[spots[0]].set(low).at[spots[1]].set(high)


def shard_levels(rng, dims, split, smallest, top_value):
    level = 1.0
    for axis_at, parts in split:
        heights = jax.random.uniform(jax.random.fold_in(jax.random.fold_in(rng, 6), axis_at), (parts,), jnp.float32, smallest / len(split), top_value / len(split))
        level = level * jnp.repeat(jnp.exp(heights), dims[axis_at] // parts).reshape((-1,) + (1,) * (len(dims) - 1 - axis_at))
    return level


def centred(stream_key, dims, scale, limit, pieces=(), held_as=jnp.bfloat16):
    values = scale * jax.random.normal(stream_key, dims, jnp.float32)
    if pieces:
        values = values * shard_levels(stream_key, dims, pieces, -0.22, 0.18)
    return jnp.clip(values, -limit, limit).astype(held_as)


def setup_inputs(seed: int = 0) -> dict:
    key_list = jax.random.split(jax.random.key(seed), 6)
    return {
        "embeddings": draw_embeddings(jax.random.fold_in(key_list[5], 71), 0),
        "fold_ids": place_ends(jax.random.randint(key_list[1], (ROWS,), 0, FOLDS), jax.random.fold_in(key_list[1], 1), 0, FOLDS - 1).astype(jnp.int32),
        "labels": place_ends(jax.random.randint(key_list[2], (ROWS,), 0, CLASSES), jax.random.fold_in(key_list[2], 1), 0, CLASSES - 1).astype(jnp.int32),
        "weights": draw_weights(jax.random.fold_in(key_list[5], 71), 0),
        "direction": centred(key_list[4], (D, COLS), D ** -0.5, 0.09375, ((0, 2), (1, 16))),
    }


def reference(embeddings, fold_ids, labels, weights, direction):
    logits = jnp.dot(embeddings, weights, preferred_element_type=jnp.float32).reshape(ROWS, CLASSES, FOLDS)
    tangent = jnp.dot(embeddings, direction, preferred_element_type=jnp.float32).reshape(ROWS, CLASSES, FOLDS)
    highest = jnp.max(logits, axis=1, keepdims=True)
    scaled = jnp.exp(logits - highest)
    summed = jnp.sum(scaled, axis=1, keepdims=True)
    moment = jnp.sum(scaled * tangent, axis=1, keepdims=True)
    probability = scaled / summed
    mean_tangent = moment / summed
    onehot = (labels[:, None] == jnp.arange(CLASSES, dtype=jnp.int32)[None, :]).astype(jnp.float32)[:, :, None]
    training = (fold_ids[:, None] != jnp.arange(FOLDS, dtype=jnp.int32)[None, :]).astype(jnp.float32)[:, None, :]
    residual_rows = (training * (probability - onehot)).reshape(ROWS, COLS).astype(jnp.bfloat16)
    curvature = (training * probability * (tangent - mean_tangent)).reshape(ROWS, COLS).astype(jnp.bfloat16)
    contract = (((0,), (0,)), ((), ()))
    gradient = lax.dot_general(embeddings, residual_rows, contract, preferred_element_type=jnp.float32)
    hess_vec = lax.dot_general(embeddings, curvature, contract, preferred_element_type=jnp.float32)
    return gradient, hess_vec
```

```python
import functools

import jax
import jax.numpy as jnp
from jax import lax
from jax.experimental import pallas as pl
from jax.experimental.pallas import tpu as pltpu
from jax.sharding import PartitionSpec as P

D = 4096
FOLDS = 5


def local(embeddings, fold_ids, labels, weights, direction):
    row_count = embeddings.shape[0]
    columns = weights.shape[1]
    per_class = columns // FOLDS
    logits = jnp.dot(
        embeddings,
        lax.all_gather(weights, "dp", axis=0, tiled=True),
        preferred_element_type=jnp.float32,
    )
    tangent = jnp.dot(
        embeddings,
        lax.all_gather(direction, "dp", axis=0, tiled=True),
        preferred_element_type=jnp.float32,
    )
    logits = logits.reshape(row_count, per_class, FOLDS)
    tangent = tangent.reshape(row_count, per_class, FOLDS)
    local_high = jnp.max(logits, axis=1)
    highest = lax.pmax(local_high, "cls")
    scaled = jnp.exp(logits - highest[:, None, :])
    summed, moment = lax.psum((jnp.sum(scaled, axis=1), jnp.sum(scaled * tangent, axis=1)), "cls")
    probability = scaled / summed[:, None, :]
    mean_tangent = moment / summed
    class_ids = lax.axis_index("cls") * per_class + jnp.arange(per_class, dtype=jnp.int32)
    onehot = (labels[:, None] == class_ids[None, :]).astype(jnp.float32)[:, :, None]
    training = (fold_ids[:, None] != jnp.arange(FOLDS, dtype=jnp.int32)[None, :]).astype(
        jnp.float32
    )[:, None, :]
    residual_rows = (
        (training * (probability - onehot)).reshape(row_count, columns).astype(jnp.bfloat16)
    )
    curvature = (
        (training * probability * (tangent - mean_tangent[:, None, :]))
        .reshape(row_count, columns)
        .astype(jnp.bfloat16)
    )
    contract = (((0,), (0,)), ((), ()))
    share = D // lax.axis_size("dp")
    full_grad, full_hvp = lax.psum(
        (
            lax.dot_general(
                embeddings, residual_rows, contract, preferred_element_type=jnp.float32
            ),
            lax.dot_general(embeddings, curvature, contract, preferred_element_type=jnp.float32),
        ),
        "dp",
    )
    offset = lax.axis_index("dp") * share
    gradient = lax.dynamic_slice_in_dim(full_grad, offset, share, 0)
    hess_vec = lax.dynamic_slice_in_dim(full_hvp, offset, share, 0)
    return (gradient, hess_vec)


MESH = pl.DeviceIdType.MESH
LANES = 128
SLOTS = FOLDS - 1
NT = (((1,), (1,)), ((), ()))


def pack(nat, base, per, fold):
    blocks = [nat[pl.ds(base + f, per, stride=FOLDS), :] for f in range(FOLDS)]
    return [jnp.where(fold > s, blocks[s], blocks[s + 1]) for s in range(SLOTS)]


def unpack(slots, nat, base, per, fold):
    for f in range(FOLDS):
        if f == 0:
            block = slots[0]
        elif f == FOLDS - 1:
            block = slots[SLOTS - 1]
        else:
            block = jnp.where(fold > f, slots[f], slots[f - 1])
        nat[pl.ds(base + f, per, stride=FOLDS), :] = jnp.where(fold == f, 0.0, block)


def merge(parts):
    high = functools.reduce(jnp.maximum, [p[0] for p in parts])
    total, moment = 0.0, 0.0
    for m, s, t in parts:
        w = jnp.exp(m - high)
        total = total + s * w
        moment = moment + t * w
    return high, total, moment


def split_stats(tile):
    return tile[0:4], tile[4:8], tile[8:12]


def exchange(
    e, wt, dt, aux, rown, rpeer, epout,
    wd, em, ep, auxp, nat, xsend, xrecv, xtot, so1, si1, so2, si2, rsend, rrecv,
    lsem, asem, ys, yr, xs, xr, c1s, c1r, c2s, c2r, ps, pr, s1s, s1r, s2s, s2r, rs, rr,
):
    rows, share = em.shape
    cols = wt.shape[0]
    per = cols // FOLDS
    packed = SLOTS * per
    quarter = share // 4
    chunks = xsend.shape[0]
    starts = [min(LANES * k, rows - LANES) for k in range(chunks)]
    pieces = [(LANES * k, min(LANES, rows - LANES * k)) for k in range(chunks)]

    d = lax.axis_index("dp")
    cls = lax.axis_index("cls")
    c = cls % 2
    x = (cls // 2) % 2
    z = cls // 4
    q = 2 * x + c
    other = 1 - d
    core = cls + 1 - 2 * c
    xn = cls + 2 - 4 * x
    group = [core, xn, cls + 3 - 2 * c - 4 * x]
    zs = [z + 1 - 2 * (z % 2), z + 2 - 4 * (z // 2), 3 - z]
    zgroup = [4 * zz + q for zz in zs]
    peer = (other, cls)

    loads = [
        pltpu.make_async_copy(wt, wd.at[pl.ds(0, cols)], lsem.at[0]),
        pltpu.make_async_copy(dt, wd.at[pl.ds(cols, cols)], lsem.at[1]),
        pltpu.make_async_copy(
            e.at[:, pl.ds(pl.multiple_of(d * share, share), share)], em, lsem.at[2]
        ),
    ]
    for load in loads:
        load.start()

    barrier = pltpu.get_barrier_semaphore()
    partners = [peer] + [(d, g) for g in group] + [(d, g) for g in zgroup]
    for partner in partners:
        pl.semaphore_signal(barrier, inc=1, device_id=partner, device_id_type=MESH)
    pl.semaphore_wait(barrier, len(partners))

    def remote(src, dst, send, recv, to):
        return pltpu.make_async_remote_copy(
            src_ref=src, dst_ref=dst, send_sem=send, recv_sem=recv,
            device_id=to, device_id_type=MESH,
        )

    qa = pl.ds(pl.multiple_of(q * quarter, quarter), quarter)
    qb = pl.ds(pl.multiple_of((q + 2 - 4 * x) * quarter, quarter), quarter)
    qs = pl.ds(pl.multiple_of(other * share + q * quarter, quarter), quarter)

    acopy = remote(aux, auxp, asem.at[0], asem.at[1], peer)
    ycopy, xcopy, c1copy, c2copy = [], [], [], []
    for t, (at, size) in enumerate(pieces):
        r = pl.ds(at, size)
        ycopy.append(remote(e.at[r, qs], ep.at[r, qa], ys.at[t], yr.at[t], peer))
        xcopy.append(remote(ep.at[r, qa], ep.at[r, qa], xs.at[t], xr.at[t], (d, xn)))
        c1copy.append(remote(ep.at[r, qa], ep.at[r, qa], c1s.at[t], c1r.at[t], (d, core)))
        c2copy.append(remote(ep.at[r, qb], ep.at[r, qb], c2s.at[t], c2r.at[t], (d, core)))
    pcopy = [remote(xsend.at[k], xrecv.at[k], ps.at[k], pr.at[k], peer) for k in range(chunks)]
    rcopy = [remote(rsend.at[k], rrecv.at[k], rs.at[k], rr.at[k], peer) for k in range(chunks)]
    s1copy = [
        [remote(so1.at[k], si1.at[k, j], s1s.at[k, j], s1r.at[k, j], (d, g)) for j, g in enumerate(group)]
        for k in range(chunks)
    ]
    s2copy = [
        [remote(so2.at[k], si2.at[k, j], s2s.at[k, j], s2r.at[k, j], (d, g)) for j, g in enumerate(zgroup)]
        for k in range(chunks)
    ]

    acopy.start()
    for copy in ycopy:
        copy.start()
    for load in loads:
        load.wait()

    def partial_slots(emb, k, fold, out):
        nat[...] = lax.dot_general(
            wd[...], emb[pl.ds(starts[k], LANES), :], NT, preferred_element_type=jnp.float32
        )
        for half in range(2):
            for s, block in enumerate(pack(nat, half * cols, per, fold)):
                out[k, pl.ds(half * packed + s * per, per), :] = block

    def stage_a(t):
        ycopy[t].wait_recv()
        xcopy[t].start()
        c1copy[t].start()

    def stage_b(t):
        xcopy[t].wait_recv()
        c2copy[t].start()

    def stage_o(k):
        partial_slots(em, k, aux[k, 0:1, :], xtot)

    def stage_c(k):
        if k == 0:
            acopy.wait_recv()
        c1copy[k].wait_recv()
        c2copy[k].wait_recv()
        partial_slots(ep, k, auxp[k, 0:1, :], xsend)
        pcopy[k].start()

    def slot(ref, k, half, s):
        return ref[k, pl.ds(half * packed + s * per, per), :]

    def stage_d(k):
        pcopy[k].wait_recv()
        xtot[k] = xtot[k] + xrecv[k]
        for s in range(SLOTS):
            logit = slot(xtot, k, 0, s)
            high = jnp.max(logit, axis=0, keepdims=True)
            scaled = jnp.exp(logit - high)
            so1[k, s : s + 1, :] = high
            so1[k, 4 + s : 5 + s, :] = jnp.sum(scaled, axis=0, keepdims=True)
            so1[k, 8 + s : 9 + s, :] = jnp.sum(scaled * slot(xtot, k, 1, s), axis=0, keepdims=True)
        so1[k, 12:16, :] = jnp.zeros((4, LANES), jnp.float32)
        for copy in s1copy[k]:
            copy.start()

    def merged(own, incoming, k):
        return merge([split_stats(own[k])] + [split_stats(incoming[k, j]) for j in range(3)])

    def stage_e(k):
        for copy in s1copy[k]:
            copy.wait_recv()
        high, total, moment = merged(so1, si1, k)
        so2[k, 0:4, :] = high
        so2[k, 4:8, :] = total
        so2[k, 8:12, :] = moment
        so2[k, 12:16, :] = jnp.zeros((4, LANES), jnp.float32)
        for copy in s2copy[k]:
            copy.start()

    def place(out, k):
        keep = starts[k] - LANES * k
        if keep:
            out[:, pl.ds(LANES * k, LANES + keep)] = nat[:, -keep:].astype(jnp.bfloat16)
        else:
            out[:, pl.ds(LANES * k, LANES)] = nat[...].astype(jnp.bfloat16)

    def stage_f(k):
        for copy in s2copy[k]:
            copy.wait_recv()
        high, total, moment = merged(so2, si2, k)
        inverse = 1.0 / total
        mean = moment * inverse
        fold, label = aux[k, 0:1, :], aux[k, 8:9, :]
        classes = lax.broadcasted_iota(jnp.int32, (per, LANES), 0) + cls * per
        onehot = jnp.where(classes.astype(jnp.float32) == label, 1.0, 0.0)
        res, cur = [], []
        for s in range(SLOTS):
            prob = jnp.exp(slot(xtot, k, 0, s) - high[s : s + 1]) * inverse[s : s + 1]
            res.append(prob - onehot)
            cur.append(prob * (slot(xtot, k, 1, s) - mean[s : s + 1]))
        for half, values in enumerate((res, cur)):
            for s, value in enumerate(values):
                rsend[k, pl.ds(half * packed + s * per, per), :] = value.astype(jnp.bfloat16)
        rcopy[k].start()
        unpack(res, nat, 0, per, fold)
        unpack(cur, nat, cols, per, fold)
        place(rown, k)

    def stage_g(k):
        rcopy[k].wait_recv()
        fold = auxp[k, 0:1, :]
        for half in range(2):
            slots = [slot(rrecv, k, half, s).astype(jnp.float32) for s in range(SLOTS)]
            unpack(slots, nat, half * cols, per, fold)
        place(rpeer, k)

    stages = {
        "a": (stage_a, 0), "b": (stage_b, 1), "c": (stage_c, 2), "o": (stage_o, 1),
        "d": (stage_d, 4), "e": (stage_e, 5), "f": (stage_f, 6), "g": (stage_g, 8),
    }
    keep = pltpu.make_async_copy(ep, epout, lsem.at[3])
    for step in range(chunks + 9):
        for name in "abcodefg":
            run, lag = stages[name]
            k = step - lag
            if 0 <= k < chunks:
                run(k)
                if name == "c" and k == chunks - 1:
                    keep.start()

    acopy.wait_send()
    for copies in (ycopy, xcopy, c1copy, c2copy, pcopy, rcopy):
        for copy in copies:
            copy.wait_send()
    for k in range(chunks):
        for copy in s1copy[k] + s2copy[k]:
            copy.wait_send()
    keep.wait()


def product(idx, rown, rpeer, em, ep, grad, hvp):
    cols = grad.shape[0]
    total = jnp.dot(rown[...], em[...], preferred_element_type=jnp.float32)
    total = total + jnp.dot(rpeer[...], ep[...], preferred_element_type=jnp.float32)
    grad[...] = total[:cols]
    hvp[...] = total[cols:]


def paired(embeddings, fold_ids, labels, weights, direction):
    rows = embeddings.shape[0]
    share, cols = weights.shape
    per = cols // FOLDS
    packed = 2 * SLOTS * per
    chunks = -(-rows // LANES)
    starts = [min(LANES * k, rows - LANES) for k in range(chunks)]
    both = jnp.stack([fold_ids, labels]).astype(jnp.float32)
    aux = jnp.stack([both[:, s : s + LANES] for s in starts])
    aux = jnp.broadcast_to(aux[:, :, None, :], (chunks, 2, 8, LANES)).reshape(chunks, 16, LANES)
    f32, bf16 = jnp.float32, jnp.bfloat16
    any_space = pl.BlockSpec(memory_space=pl.ANY)
    vmem = pl.BlockSpec(memory_space=pltpu.VMEM)
    dma = pltpu.SemaphoreType.DMA
    rown, rpeer, ep = pl.pallas_call(
        exchange,
        out_shape=(
            jax.ShapeDtypeStruct((2 * cols, rows), bf16),
            jax.ShapeDtypeStruct((2 * cols, rows), bf16),
            jax.ShapeDtypeStruct((rows, share), bf16),
        ),
        in_specs=[any_space, any_space, any_space, vmem],
        out_specs=(vmem, vmem, any_space),
        scratch_shapes=[
            pltpu.VMEM((2 * cols, share), bf16),
            pltpu.VMEM((rows, share), bf16),
            pltpu.VMEM((rows, share), bf16),
            pltpu.VMEM((chunks, 16, LANES), f32),
            pltpu.VMEM((2 * cols, LANES), f32),
            pltpu.VMEM((chunks, packed, LANES), f32),
            pltpu.VMEM((chunks, packed, LANES), f32),
            pltpu.VMEM((chunks, packed, LANES), f32),
            pltpu.VMEM((chunks, 16, LANES), f32),
            pltpu.VMEM((chunks, 3, 16, LANES), f32),
            pltpu.VMEM((chunks, 16, LANES), f32),
            pltpu.VMEM((chunks, 3, 16, LANES), f32),
            pltpu.VMEM((chunks, packed, LANES), bf16),
            pltpu.VMEM((chunks, packed, LANES), bf16),
            dma((4,)),
            dma((2,)),
        ]
        + [dma((chunks,))] * 10
        + [dma((chunks, 3))] * 4
        + [dma((chunks,))] * 2,
        compiler_params=pltpu.CompilerParams(
            collective_id=0, has_side_effects=True, vmem_limit_bytes=40 * 2**20
        ),
        name="exchange",
    )(embeddings, weights.T, direction.T, aux)

    tile = 512
    place = lax.axis_index("dp").astype(jnp.int32).reshape(1) * (share // tile)
    grad, hvp = pl.pallas_call(
        product,
        out_shape=(jax.ShapeDtypeStruct((cols, share), f32),) * 2,
        grid_spec=pltpu.PrefetchScalarGridSpec(
            num_scalar_prefetch=1,
            grid=(share // tile,),
            in_specs=[
                pl.BlockSpec((2 * cols, rows), lambda i, s: (0, 0)),
                pl.BlockSpec((2 * cols, rows), lambda i, s: (0, 0)),
                pl.BlockSpec((rows, tile), lambda i, s: (0, i + s[0])),
                pl.BlockSpec((rows, tile), lambda i, s: (0, i)),
            ],
            out_specs=(pl.BlockSpec((cols, tile), lambda i, s: (0, i)),) * 2,
        ),
        compiler_params=pltpu.CompilerParams(vmem_limit_bytes=32 * 2**20),
        name="product",
    )(place, rown, rpeer, embeddings, ep)
    return grad.T, hvp.T


def solution(mesh):
    placed = (P("dp", None), P("dp"), P("dp"), P("dp", "cls"), P("dp", "cls"))
    body = paired if mesh.shape["dp"] == 2 and mesh.shape["cls"] == 16 else local
    return jax.shard_map(
        body,
        mesh=mesh,
        in_specs=placed,
        out_specs=(P("dp", "cls"), P("dp", "cls")),
        check_vma=False,
    )
```

```python
import functools

import jax
import jax.numpy as jnp
from jax import lax
from jax.experimental import pallas as pl
from jax.experimental.pallas import tpu as pltpu
from jax.sharding import PartitionSpec as P

D = 4096
FOLDS = 5


def local(embeddings, fold_ids, labels, weights, direction):
    row_count = embeddings.shape[0]
    columns = weights.shape[1]
    per_class = columns // FOLDS
    logits = jnp.dot(
        embeddings,
        lax.all_gather(weights, "dp", axis=0, tiled=True),
        preferred_element_type=jnp.float32,
    )
    tangent = jnp.dot(
        embeddings,
        lax.all_gather(direction, "dp", axis=0, tiled=True),
        preferred_element_type=jnp.float32,
    )
    logits = logits.reshape(row_count, per_class, FOLDS)
    tangent = tangent.reshape(row_count, per_class, FOLDS)
    local_high = jnp.max(logits, axis=1)
    highest = lax.pmax(local_high, "cls")
    scaled = jnp.exp(logits - highest[:, None, :])
    summed, moment = lax.psum((jnp.sum(scaled, axis=1), jnp.sum(scaled * tangent, axis=1)), "cls")
    probability = scaled / summed[:, None, :]
    mean_tangent = moment / summed
    class_ids = lax.axis_index("cls") * per_class + jnp.arange(per_class, dtype=jnp.int32)
    onehot = (labels[:, None] == class_ids[None, :]).astype(jnp.float32)[:, :, None]
    training = (fold_ids[:, None] != jnp.arange(FOLDS, dtype=jnp.int32)[None, :]).astype(
        jnp.float32
    )[:, None, :]
    residual_rows = (
        (training * (probability - onehot)).reshape(row_count, columns).astype(jnp.bfloat16)
    )
    curvature = (
        (training * probability * (tangent - mean_tangent[:, None, :]))
        .reshape(row_count, columns)
        .astype(jnp.bfloat16)
    )
    contract = (((0,), (0,)), ((), ()))
    share = D // lax.axis_size("dp")
    full_grad, full_hvp = lax.psum(
        (
            lax.dot_general(
                embeddings, residual_rows, contract, preferred_element_type=jnp.float32
            ),
            lax.dot_general(embeddings, curvature, contract, preferred_element_type=jnp.float32),
        ),
        "dp",
    )
    offset = lax.axis_index("dp") * share
    gradient = lax.dynamic_slice_in_dim(full_grad, offset, share, 0)
    hess_vec = lax.dynamic_slice_in_dim(full_hvp, offset, share, 0)
    return (gradient, hess_vec)


MESH = pl.DeviceIdType.MESH
LANES = 128
SLOTS = FOLDS - 1
NT = (((1,), (1,)), ((), ()))


def pack(nat, base, per, fold):
    blocks = [nat[pl.ds(base + f, per, stride=FOLDS), :] for f in range(FOLDS)]
    return [jnp.where(fold > s, blocks[s], blocks[s + 1]) for s in range(SLOTS)]


def unpack(slots, nat, base, per, fold):
    for f in range(FOLDS):
        if f == 0:
            block = slots[0]
        elif f == FOLDS - 1:
            block = slots[SLOTS - 1]
        else:
            block = jnp.where(fold > f, slots[f], slots[f - 1])
        nat[pl.ds(base + f, per, stride=FOLDS), :] = jnp.where(fold == f, 0.0, block)


def merge(parts):
    high = functools.reduce(jnp.maximum, [p[0] for p in parts])
    total, moment = 0.0, 0.0
    for m, s, t in parts:
        w = jnp.exp(m - high)
        total = total + s * w
        moment = moment + t * w
    return high, total, moment


def split_stats(tile):
    return tile[0:4], tile[4:8], tile[8:12]


def exchange(
    e, wt, dt, folds, labels, partout, rpeer, epout,
    part, wd, em, ep, aux, auxp, rown, nat, xsend, xrecv, xtot, so1, si1, so2, si2, rsend, rrecv,
    lsem, asem, ys, yr, xs, xr, c1s, c1r, c2s, c2r, ps, pr, s1s, s1r, s2s, s2r, rs, rr,
):
    rows, share = em.shape
    cols = wt.shape[0]
    per = cols // FOLDS
    packed = SLOTS * per
    quarter = share // 4
    chunks = xsend.shape[0]
    starts = [min(LANES * k, rows - LANES) for k in range(chunks)]
    pieces = [(LANES * k, min(LANES, rows - LANES * k)) for k in range(chunks)]

    def halved(k):
        return starts[k] + LANES // 2 == LANES * k

    low = lax.broadcasted_iota(jnp.int32, (per, LANES), 1) < LANES // 2

    d = lax.axis_index("dp")
    cls = lax.axis_index("cls")
    c = cls % 2
    x = (cls // 2) % 2
    z = cls // 4
    q = 2 * x + c
    other = 1 - d
    core = cls + 1 - 2 * c
    xn = cls + 2 - 4 * x
    group = [core, xn, cls + 3 - 2 * c - 4 * x]
    zs = [z + 1 - 2 * (z % 2), z + 2 - 4 * (z // 2), 3 - z]
    zgroup = [4 * zz + q for zz in zs]
    peer = (other, cls)

    loads = [
        pltpu.make_async_copy(wt, wd.at[pl.ds(0, cols)], lsem.at[0]),
        pltpu.make_async_copy(dt, wd.at[pl.ds(cols, cols)], lsem.at[1]),
        pltpu.make_async_copy(
            e.at[:, pl.ds(pl.multiple_of(d * share, share), share)], em, lsem.at[2]
        ),
    ]
    barrier = pltpu.get_barrier_semaphore()
    partners = [peer] + [(d, g) for g in group] + [(d, g) for g in zgroup]
    for partner in partners:
        pl.semaphore_signal(barrier, inc=1, device_id=partner, device_id_type=MESH)
    for load in loads:
        load.start()
    for base, values in ((0, folds), (8, labels)):
        row = values[...].astype(jnp.float32).reshape(1, rows)
        for k, s in enumerate(starts):
            aux[k, base : base + 8, :] = jnp.broadcast_to(row[:, s : s + LANES], (8, LANES))
    pl.semaphore_wait(barrier, len(partners))

    def remote(src, dst, send, recv, to):
        return pltpu.make_async_remote_copy(
            src_ref=src, dst_ref=dst, send_sem=send, recv_sem=recv,
            device_id=to, device_id_type=MESH,
        )

    qa = pl.ds(pl.multiple_of(q * quarter, quarter), quarter)
    qb = pl.ds(pl.multiple_of((q + 2 - 4 * x) * quarter, quarter), quarter)
    qs = pl.ds(pl.multiple_of(other * share + q * quarter, quarter), quarter)

    acopy = remote(aux, auxp, asem.at[0], asem.at[1], peer)
    ycopy, xcopy, c1copy, c2copy = [], [], [], []
    for t, (at, size) in enumerate(pieces):
        r = pl.ds(at, size)
        ycopy.append(remote(e.at[r, qs], ep.at[r, qa], ys.at[t], yr.at[t], peer))
        xcopy.append(remote(ep.at[r, qa], ep.at[r, qa], xs.at[t], xr.at[t], (d, xn)))
        c1copy.append(remote(ep.at[r, qa], ep.at[r, qa], c1s.at[t], c1r.at[t], (d, core)))
        c2copy.append(remote(ep.at[r, qb], ep.at[r, qb], c2s.at[t], c2r.at[t], (d, core)))
    pcopy, rcopy = [], []
    for k in range(chunks):
        r = pl.ds(0, packed if halved(k) else 2 * packed)
        pcopy.append(remote(xsend.at[k, r], xrecv.at[k, r], ps.at[k], pr.at[k], peer))
        rcopy.append(remote(rsend.at[k, r], rrecv.at[k, r], rs.at[k], rr.at[k], peer))
    s1copy = [
        [remote(so1.at[k], si1.at[k, j], s1s.at[k, j], s1r.at[k, j], (d, g)) for j, g in enumerate(group)]
        for k in range(chunks)
    ]
    s2copy = [
        [remote(so2.at[k], si2.at[k, j], s2s.at[k, j], s2r.at[k, j], (d, g)) for j, g in enumerate(zgroup)]
        for k in range(chunks)
    ]

    acopy.start()
    for copy in ycopy:
        copy.start()
    for load in loads:
        load.wait()

    def partial_slots(emb, k, fold, out, joined):
        nat[...] = lax.dot_general(
            wd[...], emb[pl.ds(starts[k], LANES), :], NT, preferred_element_type=jnp.float32
        )
        store(out, k, [pack(nat, half * cols, per, fold) for half in range(2)], joined)

    def store(out, k, halves, joined):
        if joined:
            halves = [
                [jnp.where(low, pltpu.roll(b, LANES // 2, 1), a) for a, b in zip(*halves)]
            ]
        for half, blocks in enumerate(halves):
            for s, block in enumerate(blocks):
                out[k, pl.ds(half * packed + s * per, per), :] = block.astype(out.dtype)

    def received(ref, k, half, s):
        if halved(k):
            block = slot(ref, k, 0, s).astype(jnp.float32)
            return pltpu.roll(block, LANES // 2, 1) if half else block
        return slot(ref, k, half, s).astype(jnp.float32)

    def stage_a(t):
        ycopy[t].wait_recv()
        xcopy[t].start()
        c1copy[t].start()

    def stage_b(t):
        xcopy[t].wait_recv()
        c2copy[t].start()

    def stage_o(k):
        partial_slots(em, k, aux[k, 0:1, :], xtot, False)

    def stage_c(k):
        if k == 0:
            acopy.wait_recv()
        c1copy[k].wait_recv()
        c2copy[k].wait_recv()
        partial_slots(ep, k, auxp[k, 0:1, :], xsend, halved(k))
        pcopy[k].start()

    def slot(ref, k, half, s):
        return ref[k, pl.ds(half * packed + s * per, per), :]

    def stage_d(k):
        pcopy[k].wait_recv()
        for s in range(SLOTS):
            logit = slot(xtot, k, 0, s) + received(xrecv, k, 0, s)
            tangent = slot(xtot, k, 1, s) + received(xrecv, k, 1, s)
            xtot[k, pl.ds(s * per, per), :] = logit
            xtot[k, pl.ds(packed + s * per, per), :] = tangent
            high = jnp.max(logit, axis=0, keepdims=True)
            scaled = jnp.exp(logit - high)
            so1[k, s : s + 1, :] = high
            so1[k, 4 + s : 5 + s, :] = jnp.sum(scaled, axis=0, keepdims=True)
            so1[k, 8 + s : 9 + s, :] = jnp.sum(scaled * tangent, axis=0, keepdims=True)
        so1[k, 12:16, :] = jnp.zeros((4, LANES), jnp.float32)
        for copy in s1copy[k]:
            copy.start()

    def merged(own, incoming, k):
        return merge([split_stats(own[k])] + [split_stats(incoming[k, j]) for j in range(3)])

    def stage_e(k):
        for copy in s1copy[k]:
            copy.wait_recv()
        high, total, moment = merged(so1, si1, k)
        so2[k, 0:4, :] = high
        so2[k, 4:8, :] = total
        so2[k, 8:12, :] = moment
        so2[k, 12:16, :] = jnp.zeros((4, LANES), jnp.float32)
        for copy in s2copy[k]:
            copy.start()

    def place(out, k):
        keep = starts[k] - LANES * k
        if keep:
            out[:, pl.ds(LANES * k, LANES + keep)] = nat[:, -keep:].astype(jnp.bfloat16)
        else:
            out[:, pl.ds(LANES * k, LANES)] = nat[...].astype(jnp.bfloat16)

    def stage_f(k):
        for copy in s2copy[k]:
            copy.wait_recv()
        high, total, moment = merged(so2, si2, k)
        inverse = 1.0 / total
        mean = moment * inverse
        fold, label = aux[k, 0:1, :], aux[k, 8:9, :]
        classes = lax.broadcasted_iota(jnp.int32, (per, LANES), 0) + cls * per
        onehot = jnp.where(classes.astype(jnp.float32) == label, 1.0, 0.0)
        res, cur = [], []
        for s in range(SLOTS):
            prob = jnp.exp(slot(xtot, k, 0, s) - high[s : s + 1]) * inverse[s : s + 1]
            res.append(prob - onehot)
            cur.append(prob * (slot(xtot, k, 1, s) - mean[s : s + 1]))
        store(rsend, k, (res, cur), halved(k))
        unpack(res, nat, 0, per, fold)
        unpack(cur, nat, cols, per, fold)
        place(rown, k)

    def stage_g(k):
        rcopy[k].wait_recv()
        fold = auxp[k, 0:1, :]
        for half in range(2):
            slots = [received(rrecv, k, half, s) for s in range(SLOTS)]
            unpack(slots, nat, half * cols, per, fold)
        place(rpeer, k)

    keep = pltpu.make_async_copy(ep, epout, lsem.at[3])
    last = chunks - 1
    width = 512
    spans = [pl.ds(i * width, width) for i in range(share // width)]
    saves = [
        pltpu.make_async_copy(part.at[:, span], partout.at[:, span], lsem.at[4 + i])
        for i, span in enumerate(spans)
    ]

    def own_product(span, at, size):
        return jnp.dot(
            rown[:, pl.ds(at, size)], em[pl.ds(at, size), span], preferred_element_type=jnp.float32
        )

    for step in range(chunks + 2):
        for stage, lag in ((stage_a, 0), (stage_b, 1), (stage_c, 2), (stage_o, 1)):
            if 0 <= step - lag < chunks:
                stage(step - lag)
    keep.start()
    for k in range(last - 1):
        stage_d(k)
        stage_e(k)
        stage_f(k)
    stage_d(last - 1)
    stage_e(last - 1)
    stage_d(last)
    for copy in rcopy[: last - 1]:
        copy.start()
    stage_f(last - 1)
    rcopy[last - 1].start()
    stage_e(last)
    for span in spans:
        part[:, span] = own_product(span, 0, LANES * last)
    stage_f(last)
    rcopy[last].start()

    for i, span in enumerate(spans):
        part[:, span] += own_product(span, LANES * last, rows - LANES * last)
        saves[i].start()
    for k in range(chunks):
        stage_g(k)

    acopy.wait_send()
    for copies in (ycopy, xcopy, c1copy, c2copy, pcopy, rcopy):
        for copy in copies:
            copy.wait_send()
    for k in range(chunks):
        for copy in s1copy[k] + s2copy[k]:
            copy.wait_send()
    keep.wait()
    for save in saves:
        save.wait()


def product(part, rpeer, ep, grad, hvp):
    cols = grad.shape[0]
    total = part[...] + jnp.dot(rpeer[...], ep[...], preferred_element_type=jnp.float32)
    grad[...] = total[:cols]
    hvp[...] = total[cols:]


def paired(embeddings, fold_ids, labels, weights, direction):
    rows = embeddings.shape[0]
    share, cols = weights.shape
    per = cols // FOLDS
    packed = 2 * SLOTS * per
    chunks = -(-rows // LANES)
    f32, bf16 = jnp.float32, jnp.bfloat16
    hbm = pl.BlockSpec(memory_space=pltpu.HBM)
    vmem = pl.BlockSpec(memory_space=pltpu.VMEM)
    dma = pltpu.SemaphoreType.DMA
    part, rpeer, ep = pl.pallas_call(
        exchange,
        out_shape=(
            jax.ShapeDtypeStruct((2 * cols, share), f32),
            jax.ShapeDtypeStruct((2 * cols, rows), bf16),
            jax.ShapeDtypeStruct((rows, share), bf16),
        ),
        in_specs=[hbm, hbm, hbm, vmem, vmem],
        out_specs=(hbm, vmem, hbm),
        scratch_shapes=[
            pltpu.VMEM((2 * cols, share), f32),
            pltpu.VMEM((2 * cols, share), bf16),
            pltpu.VMEM((rows, share), bf16),
            pltpu.VMEM((rows, share), bf16),
            pltpu.VMEM((chunks, 16, LANES), f32),
            pltpu.VMEM((chunks, 16, LANES), f32),
            pltpu.VMEM((2 * cols, rows), bf16),
            pltpu.VMEM((2 * cols, LANES), f32),
            pltpu.VMEM((chunks, packed, LANES), f32),
            pltpu.VMEM((chunks, packed, LANES), f32),
            pltpu.VMEM((chunks, packed, LANES), f32),
            pltpu.VMEM((chunks, 16, LANES), f32),
            pltpu.VMEM((chunks, 3, 16, LANES), f32),
            pltpu.VMEM((chunks, 16, LANES), f32),
            pltpu.VMEM((chunks, 3, 16, LANES), f32),
            pltpu.VMEM((chunks, packed, LANES), bf16),
            pltpu.VMEM((chunks, packed, LANES), bf16),
            dma((4 + share // 512,)),
            dma((2,)),
        ]
        + [dma((chunks,))] * 10
        + [dma((chunks, 3))] * 4
        + [dma((chunks,))] * 2,
        compiler_params=pltpu.CompilerParams(
            collective_id=0, has_side_effects=True, vmem_limit_bytes=60 * 2**20
        ),
        name="exchange",
    )(embeddings, weights.T, direction.T, fold_ids, labels)

    tile = 512
    grad, hvp = pl.pallas_call(
        product,
        out_shape=(jax.ShapeDtypeStruct((cols, share), f32),) * 2,
        grid=(share // tile,),
        in_specs=[
            pl.BlockSpec((2 * cols, tile), lambda i: (0, i)),
            pl.BlockSpec((2 * cols, rows), lambda i: (0, 0)),
            pl.BlockSpec((rows, tile), lambda i: (0, i)),
        ],
        out_specs=(pl.BlockSpec((cols, tile), lambda i: (0, i)),) * 2,
        compiler_params=pltpu.CompilerParams(vmem_limit_bytes=60 * 2**20),
        name="product",
    )(part, rpeer, ep)
    return grad.T, hvp.T


def solution(mesh):
    placed = (P("dp", None), P("dp"), P("dp"), P("dp", "cls"), P("dp", "cls"))
    body = paired if mesh.shape["dp"] == 2 and mesh.shape["cls"] == 16 else local
    return jax.shard_map(
        body,
        mesh=mesh,
        in_specs=placed,
        out_specs=(P("dp", "cls"), P("dp", "cls")),
        check_vma=False,
    )
```

```python
import functools

import jax
import jax.numpy as jnp
from jax import lax
from jax.experimental import pallas as pl
from jax.experimental.pallas import tpu as pltpu
from jax.sharding import PartitionSpec as P

D = 4096
FOLDS = 5


def local(embeddings, fold_ids, labels, weights, direction):
    row_count = embeddings.shape[0]
    columns = weights.shape[1]
    per_class = columns // FOLDS
    logits = jnp.dot(
        embeddings,
        lax.all_gather(weights, "dp", axis=0, tiled=True),
        preferred_element_type=jnp.float32,
    )
    tangent = jnp.dot(
        embeddings,
        lax.all_gather(direction, "dp", axis=0, tiled=True),
        preferred_element_type=jnp.float32,
    )
    logits = logits.reshape(row_count, per_class, FOLDS)
    tangent = tangent.reshape(row_count, per_class, FOLDS)
    local_high = jnp.max(logits, axis=1)
    highest = lax.pmax(local_high, "cls")
    scaled = jnp.exp(logits - highest[:, None, :])
    summed, moment = lax.psum((jnp.sum(scaled, axis=1), jnp.sum(scaled * tangent, axis=1)), "cls")
    probability = scaled / summed[:, None, :]
    mean_tangent = moment / summed
    class_ids = lax.axis_index("cls") * per_class + jnp.arange(per_class, dtype=jnp.int32)
    onehot = (labels[:, None] == class_ids[None, :]).astype(jnp.float32)[:, :, None]
    training = (fold_ids[:, None] != jnp.arange(FOLDS, dtype=jnp.int32)[None, :]).astype(
        jnp.float32
    )[:, None, :]
    residual_rows = (
        (training * (probability - onehot)).reshape(row_count, columns).astype(jnp.bfloat16)
    )
    curvature = (
        (training * probability * (tangent - mean_tangent[:, None, :]))
        .reshape(row_count, columns)
        .astype(jnp.bfloat16)
    )
    contract = (((0,), (0,)), ((), ()))
    share = D // lax.axis_size("dp")
    full_grad, full_hvp = lax.psum(
        (
            lax.dot_general(
                embeddings, residual_rows, contract, preferred_element_type=jnp.float32
            ),
            lax.dot_general(embeddings, curvature, contract, preferred_element_type=jnp.float32),
        ),
        "dp",
    )
    offset = lax.axis_index("dp") * share
    gradient = lax.dynamic_slice_in_dim(full_grad, offset, share, 0)
    hess_vec = lax.dynamic_slice_in_dim(full_hvp, offset, share, 0)
    return (gradient, hess_vec)


MESH = pl.DeviceIdType.MESH
LANES = 128
SLOTS = FOLDS - 1
NT = (((1,), (1,)), ((), ()))


def pack(nat, base, per, fold):
    blocks = [nat[pl.ds(base + f, per, stride=FOLDS), :] for f in range(FOLDS)]
    return [jnp.where(fold > s, blocks[s], blocks[s + 1]) for s in range(SLOTS)]


def unpack(slots, nat, base, per, fold):
    for f in range(FOLDS):
        if f == 0:
            block = slots[0]
        elif f == FOLDS - 1:
            block = slots[SLOTS - 1]
        else:
            block = jnp.where(fold > f, slots[f], slots[f - 1])
        nat[pl.ds(base + f, per, stride=FOLDS), :] = jnp.where(fold == f, 0.0, block)


def merge(parts):
    high = functools.reduce(jnp.maximum, [p[0] for p in parts])
    total, moment = 0.0, 0.0
    for m, s, t in parts:
        w = jnp.exp(m - high)
        total = total + s * w
        moment = moment + t * w
    return high, total, moment


def split_stats(tile):
    return tile[0:4], tile[4:8], tile[8:12]


def exchange(
    e, wt, dt, folds, labels, partout, rtail, etail,
    part, wd, ee, aux, auxp, res_all, nat_own, nat_peer, xsend, xrecv, xtot, so1, si1, so2, si2, rsend, rrecv,
    lsem, asem, ys, yr, xs, xr, c1s, c1r, c2s, c2r, ps, pr, s1s, s1r, s2s, s2r, rs, rr,
):
    rows, share = ee.shape[0] // 2, ee.shape[1]
    cols = wt.shape[0]
    per = cols // FOLDS
    packed = SLOTS * per
    quarter = share // 4
    chunks = xsend.shape[0]
    pieces = [(LANES * k, min(LANES, rows - LANES * k)) for k in range(chunks)]

    def halved(k):
        return pieces[k][1] < LANES

    last = chunks - 1
    low = lax.broadcasted_iota(jnp.int32, (1, LANES), 1) < LANES // 2

    d = lax.axis_index("dp")
    cls = lax.axis_index("cls")
    c = cls % 2
    x = (cls // 2) % 2
    z = cls // 4
    q = 2 * x + c
    other = 1 - d
    core = cls + 1 - 2 * c
    xn = cls + 2 - 4 * x
    group = [core, xn, cls + 3 - 2 * c - 4 * x]
    zs = [z + 1 - 2 * (z % 2), z + 2 - 4 * (z // 2), 3 - z]
    zgroup = [4 * zz + q for zz in zs]
    peer = (other, cls)

    loads = [
        pltpu.make_async_copy(wt, wd.at[pl.ds(0, cols)], lsem.at[0]),
        pltpu.make_async_copy(dt, wd.at[pl.ds(cols, cols)], lsem.at[1]),
    ] + [
        pltpu.make_async_copy(
            e.at[pl.ds(at, size), pl.ds(pl.multiple_of(d * share, share), share)],
            ee.at[pl.ds(2 * at, size)],
            lsem.at[2 + t],
        )
        for t, (at, size) in enumerate(pieces)
    ]
    barrier = pltpu.get_barrier_semaphore()
    partners = [peer] + [(d, g) for g in group] + [(d, g) for g in zgroup]
    for partner in partners:
        pl.semaphore_signal(barrier, inc=1, device_id=partner, device_id_type=MESH)
    for load in loads:
        load.start()
    for base, values in ((0, folds), (8, labels)):
        row = values[...].astype(jnp.float32).reshape(1, rows)
        for k, (at, size) in enumerate(pieces):
            part_row = jnp.concatenate([row[:, at : at + size]] * (LANES // size), axis=1)
            aux[k, base : base + 8, :] = jnp.broadcast_to(part_row, (8, LANES))
    pl.semaphore_wait(barrier, len(partners))

    def remote(src, dst, send, recv, to):
        return pltpu.make_async_remote_copy(
            src_ref=src, dst_ref=dst, send_sem=send, recv_sem=recv,
            device_id=to, device_id_type=MESH,
        )

    qa = pl.ds(pl.multiple_of(q * quarter, quarter), quarter)
    qb = pl.ds(pl.multiple_of((q + 2 - 4 * x) * quarter, quarter), quarter)
    qs = pl.ds(pl.multiple_of(other * share + q * quarter, quarter), quarter)

    acopy = remote(aux, auxp, asem.at[0], asem.at[1], peer)
    ycopy, xcopy, c1copy, c2copy = [], [], [], []
    for t, (at, size) in enumerate(pieces):
        r = pl.ds(2 * at + size, size)
        ycopy.append(remote(e.at[pl.ds(at, size), qs], ee.at[r, qa], ys.at[t], yr.at[t], peer))
        xcopy.append(remote(ee.at[r, qa], ee.at[r, qa], xs.at[t], xr.at[t], (d, xn)))
        c1copy.append(remote(ee.at[r, qa], ee.at[r, qa], c1s.at[t], c1r.at[t], (d, core)))
        c2copy.append(remote(ee.at[r, qb], ee.at[r, qb], c2s.at[t], c2r.at[t], (d, core)))
    pcopy, rcopy = [], []
    for k in range(chunks):
        r = pl.ds(0, packed if halved(k) else 2 * packed)
        pcopy.append(remote(xsend.at[k, r], xrecv.at[k, r], ps.at[k], pr.at[k], peer))
        rcopy.append(remote(rsend.at[k, r], rrecv.at[k, r], rs.at[k], rr.at[k], peer))
    s1copy = [
        [remote(so1.at[k], si1.at[k, j], s1s.at[k, j], s1r.at[k, j], (d, g)) for j, g in enumerate(group)]
        for k in range(chunks)
    ]
    s2copy = [
        [remote(so2.at[k], si2.at[k, j], s2s.at[k, j], s2r.at[k, j], (d, g)) for j, g in enumerate(zgroup)]
        for k in range(chunks)
    ]

    acopy.start()
    for copy in ycopy:
        copy.start()

    def store(out, k, halves, first):
        if halved(k):
            joined = []
            for x0, x1 in zip(*halves):
                x1 = pltpu.roll(x1, LANES // 2, 1)
                joined.append(jnp.where(low, x0, x1) if first else jnp.where(low, x1, x0))
            halves = [joined]
        for half, blocks in enumerate(halves):
            for s, block in enumerate(blocks):
                out[k, pl.ds(half * packed + s * per, per), :] = block.astype(out.dtype)

    def received(ref, k, half, s, moved):
        if halved(k):
            block = slot(ref, k, 0, s).astype(jnp.float32)
            return pltpu.roll(block, LANES // 2, 1) if half == moved else block
        return slot(ref, k, half, s).astype(jnp.float32)

    def stage_a(t):
        ycopy[t].wait_recv()
        xcopy[t].start()
        c1copy[t].start()

    def stage_b(t):
        xcopy[t].wait_recv()
        c2copy[t].start()

    def stage_c(k):
        if k == 0:
            acopy.wait_recv()
            loads[0].wait()
            loads[1].wait()
        loads[2 + k].wait()
        c1copy[k].wait_recv()
        c2copy[k].wait_recv()
        at, size = pieces[k]
        both = lax.dot_general(
            wd[...], ee[pl.ds(2 * at, 2 * size), :], NT, preferred_element_type=jnp.float32
        )
        nat_own[...] = both[:, :LANES]
        nat_peer[...] = both[:, -LANES:]
        fold = auxp[k, 0:1, :]
        store(xsend, k, [pack(nat_peer, half * cols, per, fold) for half in range(2)], False)
        pcopy[k].start()
        fold = aux[k, 0:1, :]
        for half in range(2):
            for s, block in enumerate(pack(nat_own, half * cols, per, fold)):
                xtot[k, pl.ds(half * packed + s * per, per), :] = block

    def slot(ref, k, half, s):
        return ref[k, pl.ds(half * packed + s * per, per), :]

    def stage_d(k):
        pcopy[k].wait_recv()
        for s in range(SLOTS):
            logit = slot(xtot, k, 0, s) + received(xrecv, k, 0, s, 0)
            tangent = slot(xtot, k, 1, s) + received(xrecv, k, 1, s, 0)
            xtot[k, pl.ds(s * per, per), :] = logit
            xtot[k, pl.ds(packed + s * per, per), :] = tangent
            high = jnp.max(logit, axis=0, keepdims=True)
            scaled = jnp.exp(logit - high)
            so1[k, s : s + 1, :] = high
            so1[k, 4 + s : 5 + s, :] = jnp.sum(scaled, axis=0, keepdims=True)
            so1[k, 8 + s : 9 + s, :] = jnp.sum(scaled * tangent, axis=0, keepdims=True)
        so1[k, 12:16, :] = jnp.zeros((4, LANES), jnp.float32)
        for copy in s1copy[k]:
            copy.start()

    def merged(own, incoming, k):
        return merge([split_stats(own[k])] + [split_stats(incoming[k, j]) for j in range(3)])

    def stage_e(k):
        for copy in s1copy[k]:
            copy.wait_recv()
        high, total, moment = merged(so1, si1, k)
        so2[k, 0:4, :] = high
        so2[k, 4:8, :] = total
        so2[k, 8:12, :] = moment
        so2[k, 12:16, :] = jnp.zeros((4, LANES), jnp.float32)
        for copy in s2copy[k]:
            copy.start()

    def stage_f(k):
        for copy in s2copy[k]:
            copy.wait_recv()
        high, total, moment = merged(so2, si2, k)
        inverse = 1.0 / total
        mean = moment * inverse
        fold, label = aux[k, 0:1, :], aux[k, 8:9, :]
        classes = lax.broadcasted_iota(jnp.int32, (per, LANES), 0) + cls * per
        onehot = jnp.where(classes.astype(jnp.float32) == label, 1.0, 0.0)
        res, cur = [], []
        for s in range(SLOTS):
            prob = jnp.exp(slot(xtot, k, 0, s) - high[s : s + 1]) * inverse[s : s + 1]
            res.append(prob - onehot)
            cur.append(prob * (slot(xtot, k, 1, s) - mean[s : s + 1]))
        store(rsend, k, (res, cur), True)
        unpack(res, nat_own, 0, per, fold)
        unpack(cur, nat_own, cols, per, fold)
        if k < last:
            res_all[:, pl.ds(2 * LANES * k, LANES)] = nat_own[...].astype(jnp.bfloat16)

    def stage_g(k):
        rcopy[k].wait_recv()
        fold = auxp[k, 0:1, :]
        for half in range(2):
            slots = [received(rrecv, k, half, s, 1) for s in range(SLOTS)]
            unpack(slots, nat_peer, half * cols, per, fold)
        if k == last:
            tile = jnp.where(low, nat_own[...], pltpu.roll(nat_peer[...], LANES // 2, 1))
            rtail[:, LANES:] = tile.astype(jnp.bfloat16)
        elif k == last - 1:
            rtail[:, :LANES] = nat_peer[...].astype(jnp.bfloat16)
        else:
            res_all[:, pl.ds(2 * LANES * k + LANES, LANES)] = nat_peer[...].astype(jnp.bfloat16)

    near = res_all.shape[1]
    keep = pltpu.make_async_copy(ee.at[pl.ds(near, 2 * rows - near)], etail, lsem.at[2 + chunks])
    width = 512
    spans = [pl.ds(i * width, width) for i in range(share // width)]
    saves = [
        pltpu.make_async_copy(part.at[:, span], partout.at[:, span], lsem.at[3 + chunks + i])
        for i, span in enumerate(spans)
    ]

    def own_product(span, at, size):
        return jnp.dot(
            res_all[:, pl.ds(at, size)], ee[pl.ds(at, size), span],
            preferred_element_type=jnp.float32,
        )

    for step in range(chunks + 2):
        for stage, lag in ((stage_a, 0), (stage_b, 1), (stage_c, 2)):
            if 0 <= step - lag < chunks:
                stage(step - lag)
    keep.start()
    for k in range(last - 1):
        stage_d(k)
        stage_e(k)
        stage_f(k)
    stage_d(last - 1)
    stage_e(last - 1)
    stage_d(last)
    for copy in rcopy[: last - 1]:
        copy.start()
    stage_f(last - 1)
    rcopy[last - 1].start()
    stage_e(last)
    stage_f(last)
    rcopy[last].start()

    stage_g(0)
    stage_g(1)
    half = 4 * LANES
    for span in spans:
        part[:, span] = own_product(span, 0, half)
    for k in range(2, last - 1):
        stage_g(k)
    for i, span in enumerate(spans):
        part[:, span] += own_product(span, half, near - half)
        saves[i].start()
    stage_g(last - 1)
    stage_g(last)

    acopy.wait_send()
    for copies in (ycopy, xcopy, c1copy, c2copy, pcopy, rcopy):
        for copy in copies:
            copy.wait_send()
    for k in range(chunks):
        for copy in s1copy[k] + s2copy[k]:
            copy.wait_send()
    keep.wait()
    for save in saves:
        save.wait()


def product(part, rtail, etail, grad, hvp):
    cols = grad.shape[0]
    total = part[...] + jnp.dot(rtail[...], etail[...], preferred_element_type=jnp.float32)
    grad[...] = total[:cols]
    hvp[...] = total[cols:]


def paired(embeddings, fold_ids, labels, weights, direction):
    rows = embeddings.shape[0]
    share, cols = weights.shape
    per = cols // FOLDS
    packed = 2 * SLOTS * per
    chunks = -(-rows // LANES)
    f32, bf16 = jnp.float32, jnp.bfloat16
    hbm = pl.BlockSpec(memory_space=pltpu.HBM)
    vmem = pl.BlockSpec(memory_space=pltpu.VMEM)
    dma = pltpu.SemaphoreType.DMA
    part, rtail, etail = pl.pallas_call(
        exchange,
        out_shape=(
            jax.ShapeDtypeStruct((2 * cols, share), f32),
            jax.ShapeDtypeStruct((2 * cols, 2 * LANES), bf16),
            jax.ShapeDtypeStruct((2 * LANES, share), bf16),
        ),
        in_specs=[hbm, hbm, hbm, vmem, vmem],
        out_specs=(hbm, vmem, hbm),
        scratch_shapes=[
            pltpu.VMEM((2 * cols, share), f32),
            pltpu.VMEM((2 * cols, share), bf16),
            pltpu.VMEM((2 * rows, share), bf16),
            pltpu.VMEM((chunks, 16, LANES), f32),
            pltpu.VMEM((chunks, 16, LANES), f32),
            pltpu.VMEM((2 * cols, 2 * rows - 2 * LANES), bf16),
            pltpu.VMEM((2 * cols, LANES), f32),
            pltpu.VMEM((2 * cols, LANES), f32),
            pltpu.VMEM((chunks, packed, LANES), f32),
            pltpu.VMEM((chunks, packed, LANES), f32),
            pltpu.VMEM((chunks, packed, LANES), f32),
            pltpu.VMEM((chunks, 16, LANES), f32),
            pltpu.VMEM((chunks, 3, 16, LANES), f32),
            pltpu.VMEM((chunks, 16, LANES), f32),
            pltpu.VMEM((chunks, 3, 16, LANES), f32),
            pltpu.VMEM((chunks, packed, LANES), bf16),
            pltpu.VMEM((chunks, packed, LANES), bf16),
            dma((3 + chunks + share // 512,)),
            dma((2,)),
        ]
        + [dma((chunks,))] * 10
        + [dma((chunks, 3))] * 4
        + [dma((chunks,))] * 2,
        compiler_params=pltpu.CompilerParams(
            collective_id=0, has_side_effects=True, vmem_limit_bytes=60 * 2**20
        ),
        name="exchange",
    )(embeddings, weights.T, direction.T, fold_ids, labels)

    tile = 512
    grad, hvp = pl.pallas_call(
        product,
        out_shape=(jax.ShapeDtypeStruct((cols, share), f32),) * 2,
        grid=(share // tile,),
        in_specs=[
            pl.BlockSpec((2 * cols, tile), lambda i: (0, i)),
            pl.BlockSpec((2 * cols, 2 * LANES), lambda i: (0, 0)),
            pl.BlockSpec((2 * LANES, tile), lambda i: (0, i)),
        ],
        out_specs=(pl.BlockSpec((cols, tile), lambda i: (0, i)),) * 2,
        compiler_params=pltpu.CompilerParams(vmem_limit_bytes=60 * 2**20),
        name="product",
    )(part, rtail, etail)
    return grad.T, hvp.T


def solution(mesh):
    placed = (P("dp", None), P("dp"), P("dp"), P("dp", "cls"), P("dp", "cls"))
    body = paired if mesh.shape["dp"] == 2 and mesh.shape["cls"] == 16 else local
    return jax.shard_map(
        body,
        mesh=mesh,
        in_specs=placed,
        out_specs=(P("dp", "cls"), P("dp", "cls")),
        check_vma=False,
    )
```

```python
import functools

import jax
import jax.numpy as jnp
from jax import lax
from jax.experimental import pallas as pl
from jax.experimental.pallas import tpu as pltpu
from jax.sharding import PartitionSpec as P

D = 4096
FOLDS = 5


def local(embeddings, fold_ids, labels, weights, direction):
    row_count = embeddings.shape[0]
    columns = weights.shape[1]
    per_class = columns // FOLDS
    logits = jnp.dot(
        embeddings,
        lax.all_gather(weights, "dp", axis=0, tiled=True),
        preferred_element_type=jnp.float32,
    )
    tangent = jnp.dot(
        embeddings,
        lax.all_gather(direction, "dp", axis=0, tiled=True),
        preferred_element_type=jnp.float32,
    )
    logits = logits.reshape(row_count, per_class, FOLDS)
    tangent = tangent.reshape(row_count, per_class, FOLDS)
    local_high = jnp.max(logits, axis=1)
    highest = lax.pmax(local_high, "cls")
    scaled = jnp.exp(logits - highest[:, None, :])
    summed, moment = lax.psum((jnp.sum(scaled, axis=1), jnp.sum(scaled * tangent, axis=1)), "cls")
    probability = scaled / summed[:, None, :]
    mean_tangent = moment / summed
    class_ids = lax.axis_index("cls") * per_class + jnp.arange(per_class, dtype=jnp.int32)
    onehot = (labels[:, None] == class_ids[None, :]).astype(jnp.float32)[:, :, None]
    training = (fold_ids[:, None] != jnp.arange(FOLDS, dtype=jnp.int32)[None, :]).astype(
        jnp.float32
    )[:, None, :]
    residual_rows = (
        (training * (probability - onehot)).reshape(row_count, columns).astype(jnp.bfloat16)
    )
    curvature = (
        (training * probability * (tangent - mean_tangent[:, None, :]))
        .reshape(row_count, columns)
        .astype(jnp.bfloat16)
    )
    contract = (((0,), (0,)), ((), ()))
    share = D // lax.axis_size("dp")
    full_grad, full_hvp = lax.psum(
        (
            lax.dot_general(
                embeddings, residual_rows, contract, preferred_element_type=jnp.float32
            ),
            lax.dot_general(embeddings, curvature, contract, preferred_element_type=jnp.float32),
        ),
        "dp",
    )
    offset = lax.axis_index("dp") * share
    gradient = lax.dynamic_slice_in_dim(full_grad, offset, share, 0)
    hess_vec = lax.dynamic_slice_in_dim(full_hvp, offset, share, 0)
    return (gradient, hess_vec)


MESH = pl.DeviceIdType.MESH
LANES = 128
SLOTS = FOLDS - 1
NT = (((1,), (1,)), ((), ()))


def pack(nat, base, per, fold):
    blocks = [nat[pl.ds(base + f, per, stride=FOLDS), :] for f in range(FOLDS)]
    return [jnp.where(fold > s, blocks[s], blocks[s + 1]) for s in range(SLOTS)]


def unpack(slots, nat, base, per, fold):
    for f in range(FOLDS):
        if f == 0:
            block = slots[0]
        elif f == FOLDS - 1:
            block = slots[SLOTS - 1]
        else:
            block = jnp.where(fold > f, slots[f], slots[f - 1])
        nat[pl.ds(base + f, per, stride=FOLDS), :] = jnp.where(fold == f, 0.0, block)


def merge(parts):
    high = functools.reduce(jnp.maximum, [p[0] for p in parts])
    total, moment = 0.0, 0.0
    for m, s, t in parts:
        w = jnp.exp(m - high)
        total = total + s * w
        moment = moment + t * w
    return high, total, moment


def split_stats(tile):
    return tile[0:4], tile[4:8], tile[8:12]


def exchange(
    e, wt, dt, folds, labels, partout, rtail, etail,
    part, wd, ee, aux, auxp, res_all, nat_own, nat_peer, xsend, xrecv, xtot, so1, si1, so2, si2, rsend, rrecv,
    lsem, asem, ys, yr, xs, xr, c1s, c1r, c2s, c2r, ps, pr, s1s, s1r, s2s, s2r, rs, rr,
):
    rows, share = ee.shape[0] // 2, ee.shape[1]
    cols = wt.shape[0]
    per = cols // FOLDS
    packed = SLOTS * per
    quarter = share // 4
    chunks = xsend.shape[0]
    pieces = [(LANES * k, min(LANES, rows - LANES * k)) for k in range(chunks)]

    def halved(k):
        return pieces[k][1] < LANES

    last = chunks - 1
    low = lax.broadcasted_iota(jnp.int32, (1, LANES), 1) < LANES // 2

    d = lax.axis_index("dp")
    cls = lax.axis_index("cls")
    c = cls % 2
    x = (cls // 2) % 2
    z = cls // 4
    q = 2 * x + c
    other = 1 - d
    core = cls + 1 - 2 * c
    xn = cls + 2 - 4 * x
    group = [core, xn, cls + 3 - 2 * c - 4 * x]
    zs = [z + 1 - 2 * (z % 2), z + 2 - 4 * (z // 2), 3 - z]
    zgroup = [4 * zz + q for zz in zs]
    peer = (other, cls)

    loads = [
        pltpu.make_async_copy(wt, wd.at[pl.ds(0, cols)], lsem.at[0]),
        pltpu.make_async_copy(dt, wd.at[pl.ds(cols, cols)], lsem.at[1]),
    ] + [
        pltpu.make_async_copy(
            e.at[pl.ds(at, size), pl.ds(pl.multiple_of(d * share, share), share)],
            ee.at[pl.ds(2 * at, size)],
            lsem.at[2 + t],
        )
        for t, (at, size) in enumerate(pieces)
    ]
    barrier = pltpu.get_barrier_semaphore()
    partners = [peer] + [(d, g) for g in group] + [(d, g) for g in zgroup]
    for partner in partners:
        pl.semaphore_signal(barrier, inc=1, device_id=partner, device_id_type=MESH)
    for load in loads:
        load.start()
    for base, values in ((0, folds), (8, labels)):
        row = values[...].astype(jnp.float32).reshape(1, rows)
        for k, (at, size) in enumerate(pieces):
            part_row = jnp.concatenate([row[:, at : at + size]] * (LANES // size), axis=1)
            aux[k, base : base + 8, :] = jnp.broadcast_to(part_row, (8, LANES))
    pl.semaphore_wait(barrier, len(partners))

    def remote(src, dst, send, recv, to):
        return pltpu.make_async_remote_copy(
            src_ref=src, dst_ref=dst, send_sem=send, recv_sem=recv,
            device_id=to, device_id_type=MESH,
        )

    qa = pl.ds(pl.multiple_of(q * quarter, quarter), quarter)
    qb = pl.ds(pl.multiple_of((q + 2 - 4 * x) * quarter, quarter), quarter)
    qs = pl.ds(pl.multiple_of(other * share + q * quarter, quarter), quarter)

    acopy = remote(aux, auxp, asem.at[0], asem.at[1], peer)
    ycopy, xcopy, c1copy, c2copy = [], [], [], []
    for t, (at, size) in enumerate(pieces):
        r = pl.ds(2 * at + size, size)
        ycopy.append(remote(e.at[pl.ds(at, size), qs], ee.at[r, qa], ys.at[t], yr.at[t], peer))
        xcopy.append(remote(ee.at[r, qa], ee.at[r, qa], xs.at[t], xr.at[t], (d, xn)))
        c1copy.append(remote(ee.at[r, qa], ee.at[r, qa], c1s.at[t], c1r.at[t], (d, core)))
        c2copy.append(remote(ee.at[r, qb], ee.at[r, qb], c2s.at[t], c2r.at[t], (d, core)))
    pcopy, rcopy = [], []
    for k in range(chunks):
        r = pl.ds(0, packed if halved(k) else 2 * packed)
        pcopy.append(remote(xsend.at[k, r], xrecv.at[k, r], ps.at[k], pr.at[k], peer))
        rcopy.append(remote(rsend.at[k, r], rrecv.at[k, r], rs.at[k], rr.at[k], peer))
    s1copy = [
        [remote(so1.at[k], si1.at[k, j], s1s.at[k, j], s1r.at[k, j], (d, g)) for j, g in enumerate(group)]
        for k in range(chunks)
    ]
    s2copy = [
        [remote(so2.at[k], si2.at[k, j], s2s.at[k, j], s2r.at[k, j], (d, g)) for j, g in enumerate(zgroup)]
        for k in range(chunks)
    ]

    acopy.start()
    for copy in ycopy:
        copy.start()

    def store(out, k, halves, first):
        if halved(k):
            joined = []
            for x0, x1 in zip(*halves):
                x1 = pltpu.roll(x1, LANES // 2, 1)
                joined.append(jnp.where(low, x0, x1) if first else jnp.where(low, x1, x0))
            halves = [joined]
        for half, blocks in enumerate(halves):
            for s, block in enumerate(blocks):
                out[k, pl.ds(half * packed + s * per, per), :] = block.astype(out.dtype)

    def received(ref, k, half, s, moved):
        if halved(k):
            block = slot(ref, k, 0, s).astype(jnp.float32)
            return pltpu.roll(block, LANES // 2, 1) if half == moved else block
        return slot(ref, k, half, s).astype(jnp.float32)

    def stage_a(t):
        ycopy[t].wait_recv()
        xcopy[t].start()
        c1copy[t].start()

    def stage_b(t):
        xcopy[t].wait_recv()
        c2copy[t].start()

    def stage_c(k):
        if k == 0:
            acopy.wait_recv()
            loads[0].wait()
            loads[1].wait()
        loads[2 + k].wait()
        c1copy[k].wait_recv()
        c2copy[k].wait_recv()
        at, size = pieces[k]
        both = lax.dot_general(
            wd[...], ee[pl.ds(2 * at, 2 * size), :], NT, preferred_element_type=jnp.float32
        )
        nat_own[...] = both[:, :LANES]
        nat_peer[...] = both[:, -LANES:]
        fold = auxp[k, 0:1, :]
        store(xsend, k, [pack(nat_peer, half * cols, per, fold) for half in range(2)], False)
        pcopy[k].start()
        fold = aux[k, 0:1, :]
        for half in range(2):
            for s, block in enumerate(pack(nat_own, half * cols, per, fold)):
                xtot[k, pl.ds(half * packed + s * per, per), :] = block

    def slot(ref, k, half, s):
        return ref[k, pl.ds(half * packed + s * per, per), :]

    def stage_d(k):
        pcopy[k].wait_recv()
        for s in range(SLOTS):
            logit = slot(xtot, k, 0, s) + received(xrecv, k, 0, s, 0)
            tangent = slot(xtot, k, 1, s) + received(xrecv, k, 1, s, 0)
            xtot[k, pl.ds(s * per, per), :] = logit
            xtot[k, pl.ds(packed + s * per, per), :] = tangent
            high = jnp.max(logit, axis=0, keepdims=True)
            scaled = jnp.exp(logit - high)
            so1[k, s : s + 1, :] = high
            so1[k, 4 + s : 5 + s, :] = jnp.sum(scaled, axis=0, keepdims=True)
            so1[k, 8 + s : 9 + s, :] = jnp.sum(scaled * tangent, axis=0, keepdims=True)
        so1[k, 12:16, :] = jnp.zeros((4, LANES), jnp.float32)
        for copy in s1copy[k]:
            copy.start()

    def merged(own, incoming, k):
        return merge([split_stats(own[k])] + [split_stats(incoming[k, j]) for j in range(3)])

    def stage_e(k):
        for copy in s1copy[k]:
            copy.wait_recv()
        high, total, moment = merged(so1, si1, k)
        so2[k, 0:4, :] = high
        so2[k, 4:8, :] = total
        so2[k, 8:12, :] = moment
        so2[k, 12:16, :] = jnp.zeros((4, LANES), jnp.float32)
        for copy in s2copy[k]:
            copy.start()

    def stage_f(k):
        for copy in s2copy[k]:
            copy.wait_recv()
        high, total, moment = merged(so2, si2, k)
        inverse = 1.0 / total
        mean = moment * inverse
        fold, label = aux[k, 0:1, :], aux[k, 8:9, :]
        classes = lax.broadcasted_iota(jnp.int32, (per, LANES), 0) + cls * per
        onehot = jnp.where(classes.astype(jnp.float32) == label, 1.0, 0.0)
        res, cur = [], []
        for s in range(SLOTS):
            prob = jnp.exp(slot(xtot, k, 0, s) - high[s : s + 1]) * inverse[s : s + 1]
            res.append(prob - onehot)
            cur.append(prob * (slot(xtot, k, 1, s) - mean[s : s + 1]))
        store(rsend, k, (res, cur), True)
        unpack(res, nat_own, 0, per, fold)
        unpack(cur, nat_own, cols, per, fold)
        if k < last:
            res_all[:, pl.ds(2 * LANES * k, LANES)] = nat_own[...].astype(jnp.bfloat16)

    def stage_g(k):
        rcopy[k].wait_recv()
        fold = auxp[k, 0:1, :]
        for half in range(2):
            slots = [received(rrecv, k, half, s, 1) for s in range(SLOTS)]
            unpack(slots, nat_peer, half * cols, per, fold)
        if k == last:
            tile = jnp.where(low, nat_own[...], pltpu.roll(nat_peer[...], LANES // 2, 1))
            rtail[:, LANES:] = tile.astype(jnp.bfloat16)
        elif k == last - 1:
            rtail[:, :LANES] = nat_peer[...].astype(jnp.bfloat16)
        else:
            res_all[:, pl.ds(2 * LANES * k + LANES, LANES)] = nat_peer[...].astype(jnp.bfloat16)

    near = res_all.shape[1]
    keep = pltpu.make_async_copy(ee.at[pl.ds(near, 2 * rows - near)], etail, lsem.at[2 + chunks])
    width = 512
    spans = [pl.ds(i * width, width) for i in range(share // width)]
    saves = [
        pltpu.make_async_copy(part.at[:, span], partout.at[:, span], lsem.at[3 + chunks + i])
        for i, span in enumerate(spans)
    ]

    def own_product(span, at, size):
        return jnp.dot(
            res_all[:, pl.ds(at, size)], ee[pl.ds(at, size), span],
            preferred_element_type=jnp.float32,
        )

    for step in range(chunks + 2):
        for stage, lag in ((stage_a, 0), (stage_b, 1), (stage_c, 2)):
            if 0 <= step - lag < chunks:
                stage(step - lag)
    keep.start()
    for step in range(chunks + 2):
        if step <= last:
            stage_d(step)
        if step == last:
            for copy in rcopy[: last - 2]:
                copy.start()
        if 0 <= step - 1 <= last:
            stage_e(step - 1)
        if 0 <= step - 2 <= last:
            stage_f(step - 2)
            if step - 2 >= last - 2:
                rcopy[step - 2].start()

    stage_g(0)
    stage_g(1)
    half = 4 * LANES
    for span in spans:
        part[:, span] = own_product(span, 0, half)
    for k in range(2, last - 1):
        stage_g(k)
    for i, span in enumerate(spans):
        part[:, span] += own_product(span, half, near - half)
        saves[i].start()
    stage_g(last - 1)
    stage_g(last)

    acopy.wait_send()
    for copies in (ycopy, xcopy, c1copy, c2copy, pcopy, rcopy):
        for copy in copies:
            copy.wait_send()
    for k in range(chunks):
        for copy in s1copy[k] + s2copy[k]:
            copy.wait_send()
    keep.wait()
    for save in saves:
        save.wait()


def product(part, rtail, etail, grad, hvp):
    cols = grad.shape[0]
    total = part[...] + jnp.dot(rtail[...], etail[...], preferred_element_type=jnp.float32)
    grad[...] = total[:cols]
    hvp[...] = total[cols:]


def paired(embeddings, fold_ids, labels, weights, direction):
    rows = embeddings.shape[0]
    share, cols = weights.shape
    per = cols // FOLDS
    packed = 2 * SLOTS * per
    chunks = -(-rows // LANES)
    f32, bf16 = jnp.float32, jnp.bfloat16
    hbm = pl.BlockSpec(memory_space=pltpu.HBM)
    vmem = pl.BlockSpec(memory_space=pltpu.VMEM)
    dma = pltpu.SemaphoreType.DMA
    part, rtail, etail = pl.pallas_call(
        exchange,
        out_shape=(
            jax.ShapeDtypeStruct((2 * cols, share), f32),
            jax.ShapeDtypeStruct((2 * cols, 2 * LANES), bf16),
            jax.ShapeDtypeStruct((2 * LANES, share), bf16),
        ),
        in_specs=[hbm, hbm, hbm, vmem, vmem],
        out_specs=(hbm, vmem, hbm),
        scratch_shapes=[
            pltpu.VMEM((2 * cols, share), f32),
            pltpu.VMEM((2 * cols, share), bf16),
            pltpu.VMEM((2 * rows, share), bf16),
            pltpu.VMEM((chunks, 16, LANES), f32),
            pltpu.VMEM((chunks, 16, LANES), f32),
            pltpu.VMEM((2 * cols, 2 * rows - 2 * LANES), bf16),
            pltpu.VMEM((2 * cols, LANES), f32),
            pltpu.VMEM((2 * cols, LANES), f32),
            pltpu.VMEM((chunks, packed, LANES), f32),
            pltpu.VMEM((chunks, packed, LANES), f32),
            pltpu.VMEM((chunks, packed, LANES), f32),
            pltpu.VMEM((chunks, 16, LANES), f32),
            pltpu.VMEM((chunks, 3, 16, LANES), f32),
            pltpu.VMEM((chunks, 16, LANES), f32),
            pltpu.VMEM((chunks, 3, 16, LANES), f32),
            pltpu.VMEM((chunks, packed, LANES), bf16),
            pltpu.VMEM((chunks, packed, LANES), bf16),
            dma((3 + chunks + share // 512,)),
            dma((2,)),
        ]
        + [dma((chunks,))] * 10
        + [dma((chunks, 3))] * 4
        + [dma((chunks,))] * 2,
        compiler_params=pltpu.CompilerParams(
            collective_id=0, has_side_effects=True, vmem_limit_bytes=60 * 2**20
        ),
        name="exchange",
    )(embeddings, weights.T, direction.T, fold_ids, labels)

    tile = 512
    grad, hvp = pl.pallas_call(
        product,
        out_shape=(jax.ShapeDtypeStruct((cols, share), f32),) * 2,
        grid=(share // tile,),
        in_specs=[
            pl.BlockSpec((2 * cols, tile), lambda i: (0, i)),
            pl.BlockSpec((2 * cols, 2 * LANES), lambda i: (0, 0)),
            pl.BlockSpec((2 * LANES, tile), lambda i: (0, i)),
        ],
        out_specs=(pl.BlockSpec((cols, tile), lambda i: (0, i)),) * 2,
        compiler_params=pltpu.CompilerParams(vmem_limit_bytes=60 * 2**20),
        name="product",
    )(part, rtail, etail)
    return grad.T, hvp.T


def solution(mesh):
    placed = (P("dp", None), P("dp"), P("dp"), P("dp", "cls"), P("dp", "cls"))
    body = paired if mesh.shape["dp"] == 2 and mesh.shape["cls"] == 16 else local
    return jax.shard_map(
        body,
        mesh=mesh,
        in_specs=placed,
        out_specs=(P("dp", "cls"), P("dp", "cls")),
        check_vma=False,
    )
```

```python
import functools

import jax
import jax.numpy as jnp
from jax import lax
from jax.experimental import pallas as pl
from jax.experimental.pallas import tpu as pltpu
from jax.sharding import PartitionSpec as P

D = 4096
FOLDS = 5


def local(embeddings, fold_ids, labels, weights, direction):
    row_count = embeddings.shape[0]
    columns = weights.shape[1]
    per_class = columns // FOLDS
    logits = jnp.dot(
        embeddings,
        lax.all_gather(weights, "dp", axis=0, tiled=True),
        preferred_element_type=jnp.float32,
    )
    tangent = jnp.dot(
        embeddings,
        lax.all_gather(direction, "dp", axis=0, tiled=True),
        preferred_element_type=jnp.float32,
    )
    logits = logits.reshape(row_count, per_class, FOLDS)
    tangent = tangent.reshape(row_count, per_class, FOLDS)
    local_high = jnp.max(logits, axis=1)
    highest = lax.pmax(local_high, "cls")
    scaled = jnp.exp(logits - highest[:, None, :])
    summed, moment = lax.psum((jnp.sum(scaled, axis=1), jnp.sum(scaled * tangent, axis=1)), "cls")
    probability = scaled / summed[:, None, :]
    mean_tangent = moment / summed
    class_ids = lax.axis_index("cls") * per_class + jnp.arange(per_class, dtype=jnp.int32)
    onehot = (labels[:, None] == class_ids[None, :]).astype(jnp.float32)[:, :, None]
    training = (fold_ids[:, None] != jnp.arange(FOLDS, dtype=jnp.int32)[None, :]).astype(
        jnp.float32
    )[:, None, :]
    residual_rows = (
        (training * (probability - onehot)).reshape(row_count, columns).astype(jnp.bfloat16)
    )
    curvature = (
        (training * probability * (tangent - mean_tangent[:, None, :]))
        .reshape(row_count, columns)
        .astype(jnp.bfloat16)
    )
    contract = (((0,), (0,)), ((), ()))
    share = D // lax.axis_size("dp")
    full_grad, full_hvp = lax.psum(
        (
            lax.dot_general(
                embeddings, residual_rows, contract, preferred_element_type=jnp.float32
            ),
            lax.dot_general(embeddings, curvature, contract, preferred_element_type=jnp.float32),
        ),
        "dp",
    )
    offset = lax.axis_index("dp") * share
    gradient = lax.dynamic_slice_in_dim(full_grad, offset, share, 0)
    hess_vec = lax.dynamic_slice_in_dim(full_hvp, offset, share, 0)
    return (gradient, hess_vec)


MESH = pl.DeviceIdType.MESH
LANES = 128
SLOTS = FOLDS - 1
NT = (((1,), (1,)), ((), ()))


def pack(nat, base, per, fold):
    blocks = [nat[pl.ds(base + f, per, stride=FOLDS), :] for f in range(FOLDS)]
    return [jnp.where(fold > s, blocks[s], blocks[s + 1]) for s in range(SLOTS)]


def unpack(slots, nat, base, per, fold):
    for f in range(FOLDS):
        if f == 0:
            block = slots[0]
        elif f == FOLDS - 1:
            block = slots[SLOTS - 1]
        else:
            block = jnp.where(fold > f, slots[f], slots[f - 1])
        nat[pl.ds(base + f, per, stride=FOLDS), :] = jnp.where(fold == f, 0.0, block)


def merge(parts):
    high = functools.reduce(jnp.maximum, [p[0] for p in parts])
    total, moment = 0.0, 0.0
    for m, s, t in parts:
        w = jnp.exp(m - high)
        total = total + s * w
        moment = moment + t * w
    return high, total, moment


def split_stats(tile):
    return tile[0:4], tile[4:8], tile[8:12]


def exchange(
    e, wt, dt, folds, labels, partout, rtail, etail,
    part, wd, ee, aux, auxp, res_all, nat_own, nat_peer, xsend, xrecv, xtot, so1, si1, so2, si2, rsend, rrecv,
    lsem, asem, hs, hr, ps, pr, s1s, s1r, s2s, s2r, rs, rr,
):
    rows, share = ee.shape[0] // 2, ee.shape[1]
    cols = wt.shape[0]
    per = cols // FOLDS
    packed = SLOTS * per
    eighth = share // 8
    chunks = xsend.shape[0]
    pieces = [(LANES * k, min(LANES, rows - LANES * k)) for k in range(chunks)]

    def halved(k):
        return pieces[k][1] < LANES

    last = chunks - 1
    low = lax.broadcasted_iota(jnp.int32, (1, LANES), 1) < LANES // 2

    d = lax.axis_index("dp")
    cls = lax.axis_index("cls")
    c = cls % 2
    x = (cls // 2) % 2
    z = cls // 4
    q = 2 * x + c
    other = 1 - d
    core = cls + 1 - 2 * c
    xn = cls + 2 - 4 * x
    group = [core, xn, cls + 3 - 2 * c - 4 * x]
    zs = [z + 1 - 2 * (z % 2), z + 2 - 4 * (z // 2), 3 - z]
    zgroup = [4 * zz + q for zz in zs]
    peer = (other, cls)

    loads = [
        pltpu.make_async_copy(wt, wd.at[pl.ds(0, cols)], lsem.at[0]),
        pltpu.make_async_copy(dt, wd.at[pl.ds(cols, cols)], lsem.at[1]),
    ] + [
        pltpu.make_async_copy(
            e.at[pl.ds(at, size), pl.ds(pl.multiple_of(d * share, share), share)],
            ee.at[pl.ds(2 * at, size)],
            lsem.at[2 + t],
        )
        for t, (at, size) in enumerate(pieces)
    ]
    barrier = pltpu.get_barrier_semaphore()
    partners = [peer] + [(d, g) for g in group] + [(d, g) for g in zgroup]
    for partner in partners:
        pl.semaphore_signal(barrier, inc=1, device_id=partner, device_id_type=MESH)
    for load in loads:
        load.start()
    for base, values in ((0, folds), (8, labels)):
        row = values[...].astype(jnp.float32).reshape(1, rows)
        for k, (at, size) in enumerate(pieces):
            part_row = jnp.concatenate([row[:, at : at + size]] * (LANES // size), axis=1)
            aux[k, base : base + 8, :] = jnp.broadcast_to(part_row, (8, LANES))
    pl.semaphore_wait(barrier, len(partners))

    def remote(src, dst, send, recv, to):
        return pltpu.make_async_remote_copy(
            src_ref=src, dst_ref=dst, send_sem=send, recv_sem=recv,
            device_id=to, device_id_type=MESH,
        )

    zz = z % 2
    zn = cls + 4 - 8 * zz
    p = 4 * zz + q

    def piece(index, base=0):
        return pl.ds(pl.multiple_of(base + index * eighth, eighth), eighth)

    px, pz = p + 2 - 4 * x, p + 4 - 8 * zz
    pd = px + 4 - 8 * zz
    pf = (1 - c) * px + c * pz
    to_diag = (1 - c) * zn + c * xn

    acopy = remote(aux, auxp, asem.at[0], asem.at[1], peer)
    hops = []
    for t, (at, size) in enumerate(pieces):
        r = pl.ds(2 * at + size, size)
        routes = [(p, xn), (p, zn), (p, core), (pf, to_diag), (px, core), (pz, core), (pd, core)]
        hop = [
            remote(
                e.at[pl.ds(at, size), piece(p, other * share)], ee.at[r, piece(p)],
                hs.at[0, t], hr.at[0, t], peer,
            )
        ]
        for j, (index, to) in enumerate(routes):
            block = ee.at[r, piece(index)]
            hop.append(remote(block, block, hs.at[j + 1, t], hr.at[j + 1, t], (d, to)))
        hops.append(hop)
    pcopy, rcopy = [], []
    for k in range(chunks):
        r = pl.ds(0, packed if halved(k) else 2 * packed)
        pcopy.append(remote(xsend.at[k, r], xrecv.at[k, r], ps.at[k], pr.at[k], peer))
        rcopy.append(remote(rsend.at[k, r], rrecv.at[k, r], rs.at[k], rr.at[k], peer))
    s1copy = [
        [remote(so1.at[k], si1.at[k, j], s1s.at[k, j], s1r.at[k, j], (d, g)) for j, g in enumerate(group)]
        for k in range(chunks)
    ]
    s2copy = [
        [remote(so2.at[k], si2.at[k, j], s2s.at[k, j], s2r.at[k, j], (d, g)) for j, g in enumerate(zgroup)]
        for k in range(chunks)
    ]

    acopy.start()
    for hop in hops:
        hop[0].start()

    def store(out, k, halves, first):
        if halved(k):
            joined = []
            for x0, x1 in zip(*halves):
                x1 = pltpu.roll(x1, LANES // 2, 1)
                joined.append(jnp.where(low, x0, x1) if first else jnp.where(low, x1, x0))
            halves = [joined]
        for half, blocks in enumerate(halves):
            for s, block in enumerate(blocks):
                out[k, pl.ds(half * packed + s * per, per), :] = block.astype(out.dtype)

    def received(ref, k, half, s, moved):
        if halved(k):
            block = slot(ref, k, 0, s).astype(jnp.float32)
            return pltpu.roll(block, LANES // 2, 1) if half == moved else block
        return slot(ref, k, half, s).astype(jnp.float32)

    def stage_a(t):
        hops[t][0].wait_recv()
        for j in (1, 2, 3):
            hops[t][j].start()

    def stage_b(t):
        hops[t][1].wait_recv()
        hops[t][2].wait_recv()
        for j in (4, 5, 6):
            hops[t][j].start()

    def stage_x(t):
        hops[t][4].wait_recv()
        hops[t][7].start()

    def stage_c(k):
        if k == 0:
            acopy.wait_recv()
            loads[0].wait()
            loads[1].wait()
        loads[2 + k].wait()
        for j in (3, 5, 6, 7):
            hops[k][j].wait_recv()
        at, size = pieces[k]
        both = lax.dot_general(
            wd[...], ee[pl.ds(2 * at, 2 * size), :], NT, preferred_element_type=jnp.float32
        )
        nat_own[...] = both[:, :LANES]
        nat_peer[...] = both[:, -LANES:]
        fold = auxp[k, 0:1, :]
        store(xsend, k, [pack(nat_peer, half * cols, per, fold) for half in range(2)], False)
        pcopy[k].start()
        fold = aux[k, 0:1, :]
        for half in range(2):
            for s, block in enumerate(pack(nat_own, half * cols, per, fold)):
                xtot[k, pl.ds(half * packed + s * per, per), :] = block

    def slot(ref, k, half, s):
        return ref[k, pl.ds(half * packed + s * per, per), :]

    def stage_d(k):
        pcopy[k].wait_recv()
        for s in range(SLOTS):
            logit = slot(xtot, k, 0, s) + received(xrecv, k, 0, s, 0)
            tangent = slot(xtot, k, 1, s) + received(xrecv, k, 1, s, 0)
            xtot[k, pl.ds(s * per, per), :] = logit
            xtot[k, pl.ds(packed + s * per, per), :] = tangent
            high = jnp.max(logit, axis=0, keepdims=True)
            scaled = jnp.exp(logit - high)
            so1[k, s : s + 1, :] = high
            so1[k, 4 + s : 5 + s, :] = jnp.sum(scaled, axis=0, keepdims=True)
            so1[k, 8 + s : 9 + s, :] = jnp.sum(scaled * tangent, axis=0, keepdims=True)
        so1[k, 12:16, :] = jnp.zeros((4, LANES), jnp.float32)
        for copy in s1copy[k]:
            copy.start()

    def merged(own, incoming, k):
        return merge([split_stats(own[k])] + [split_stats(incoming[k, j]) for j in range(3)])

    def stage_e(k):
        for copy in s1copy[k]:
            copy.wait_recv()
        high, total, moment = merged(so1, si1, k)
        so2[k, 0:4, :] = high
        so2[k, 4:8, :] = total
        so2[k, 8:12, :] = moment
        so2[k, 12:16, :] = jnp.zeros((4, LANES), jnp.float32)
        for copy in s2copy[k]:
            copy.start()

    def stage_f(k):
        for copy in s2copy[k]:
            copy.wait_recv()
        high, total, moment = merged(so2, si2, k)
        inverse = 1.0 / total
        mean = moment * inverse
        fold, label = aux[k, 0:1, :], aux[k, 8:9, :]
        classes = lax.broadcasted_iota(jnp.int32, (per, LANES), 0) + cls * per
        onehot = jnp.where(classes.astype(jnp.float32) == label, 1.0, 0.0)
        res, cur = [], []
        for s in range(SLOTS):
            prob = jnp.exp(slot(xtot, k, 0, s) - high[s : s + 1]) * inverse[s : s + 1]
            res.append(prob - onehot)
            cur.append(prob * (slot(xtot, k, 1, s) - mean[s : s + 1]))
        store(rsend, k, (res, cur), True)
        unpack(res, nat_own, 0, per, fold)
        unpack(cur, nat_own, cols, per, fold)
        if k < last:
            res_all[:, pl.ds(2 * LANES * k, LANES)] = nat_own[...].astype(jnp.bfloat16)

    def stage_g(k):
        rcopy[k].wait_recv()
        fold = auxp[k, 0:1, :]
        for half in range(2):
            slots = [received(rrecv, k, half, s, 1) for s in range(SLOTS)]
            unpack(slots, nat_peer, half * cols, per, fold)
        if k == last:
            tile = jnp.where(low, nat_own[...], pltpu.roll(nat_peer[...], LANES // 2, 1))
            rtail[:, LANES:] = tile.astype(jnp.bfloat16)
        elif k == last - 1:
            rtail[:, :LANES] = nat_peer[...].astype(jnp.bfloat16)
        else:
            res_all[:, pl.ds(2 * LANES * k + LANES, LANES)] = nat_peer[...].astype(jnp.bfloat16)

    near = res_all.shape[1]
    keep = pltpu.make_async_copy(ee.at[pl.ds(near, 2 * rows - near)], etail, lsem.at[2 + chunks])
    width = 512
    spans = [pl.ds(i * width, width) for i in range(share // width)]
    saves = [
        pltpu.make_async_copy(part.at[:, span], partout.at[:, span], lsem.at[3 + chunks + i])
        for i, span in enumerate(spans)
    ]

    def own_product(span, at, size):
        return jnp.dot(
            res_all[:, pl.ds(at, size)], ee[pl.ds(at, size), span],
            preferred_element_type=jnp.float32,
        )

    for step in range(chunks + 3):
        for stage, lag in ((stage_a, 0), (stage_b, 1), (stage_x, 2), (stage_c, 3)):
            if 0 <= step - lag < chunks:
                stage(step - lag)
    keep.start()
    for step in range(chunks + 2):
        if step <= last:
            stage_d(step)
        if step == last:
            for copy in rcopy[: last - 2]:
                copy.start()
        if 0 <= step - 1 <= last:
            stage_e(step - 1)
        if 0 <= step - 2 <= last:
            stage_f(step - 2)
            if step - 2 >= last - 2:
                rcopy[step - 2].start()

    stage_g(0)
    stage_g(1)
    half = 4 * LANES
    for span in spans:
        part[:, span] = own_product(span, 0, half)
    for k in range(2, last - 1):
        stage_g(k)
    for i, span in enumerate(spans):
        part[:, span] += own_product(span, half, near - half)
        saves[i].start()
    stage_g(last - 1)
    stage_g(last)

    acopy.wait_send()
    for copies in hops + [pcopy, rcopy]:
        for copy in copies:
            copy.wait_send()
    for k in range(chunks):
        for copy in s1copy[k] + s2copy[k]:
            copy.wait_send()
    keep.wait()
    for save in saves:
        save.wait()


def product(part, rtail, etail, grad, hvp):
    cols = grad.shape[0]
    total = part[...] + jnp.dot(rtail[...], etail[...], preferred_element_type=jnp.float32)
    grad[...] = total[:cols]
    hvp[...] = total[cols:]


def paired(embeddings, fold_ids, labels, weights, direction):
    rows = embeddings.shape[0]
    share, cols = weights.shape
    per = cols // FOLDS
    packed = 2 * SLOTS * per
    chunks = -(-rows // LANES)
    f32, bf16 = jnp.float32, jnp.bfloat16
    hbm = pl.BlockSpec(memory_space=pltpu.HBM)
    vmem = pl.BlockSpec(memory_space=pltpu.VMEM)
    dma = pltpu.SemaphoreType.DMA
    part, rtail, etail = pl.pallas_call(
        exchange,
        out_shape=(
            jax.ShapeDtypeStruct((2 * cols, share), f32),
            jax.ShapeDtypeStruct((2 * cols, 2 * LANES), bf16),
            jax.ShapeDtypeStruct((2 * LANES, share), bf16),
        ),
        in_specs=[hbm, hbm, hbm, vmem, vmem],
        out_specs=(hbm, vmem, hbm),
        scratch_shapes=[
            pltpu.VMEM((2 * cols, share), f32),
            pltpu.VMEM((2 * cols, share), bf16),
            pltpu.VMEM((2 * rows, share), bf16),
            pltpu.VMEM((chunks, 16, LANES), f32),
            pltpu.VMEM((chunks, 16, LANES), f32),
            pltpu.VMEM((2 * cols, 2 * rows - 2 * LANES), bf16),
            pltpu.VMEM((2 * cols, LANES), f32),
            pltpu.VMEM((2 * cols, LANES), f32),
            pltpu.VMEM((chunks, packed, LANES), f32),
            pltpu.VMEM((chunks, packed, LANES), f32),
            pltpu.VMEM((chunks, packed, LANES), f32),
            pltpu.VMEM((chunks, 16, LANES), f32),
            pltpu.VMEM((chunks, 3, 16, LANES), f32),
            pltpu.VMEM((chunks, 16, LANES), f32),
            pltpu.VMEM((chunks, 3, 16, LANES), f32),
            pltpu.VMEM((chunks, packed, LANES), bf16),
            pltpu.VMEM((chunks, packed, LANES), bf16),
            dma((3 + chunks + share // 512,)),
            dma((2,)),
        ]
        + [dma((8, chunks))] * 2
        + [dma((chunks,))] * 2
        + [dma((chunks, 3))] * 4
        + [dma((chunks,))] * 2,
        compiler_params=pltpu.CompilerParams(
            collective_id=0, has_side_effects=True, vmem_limit_bytes=60 * 2**20
        ),
        name="exchange",
    )(embeddings, weights.T, direction.T, fold_ids, labels)

    tile = 512
    grad, hvp = pl.pallas_call(
        product,
        out_shape=(jax.ShapeDtypeStruct((cols, share), f32),) * 2,
        grid=(share // tile,),
        in_specs=[
            pl.BlockSpec((2 * cols, tile), lambda i: (0, i)),
            pl.BlockSpec((2 * cols, 2 * LANES), lambda i: (0, 0)),
            pl.BlockSpec((2 * LANES, tile), lambda i: (0, i)),
        ],
        out_specs=(pl.BlockSpec((cols, tile), lambda i: (0, i)),) * 2,
        compiler_params=pltpu.CompilerParams(vmem_limit_bytes=60 * 2**20),
        name="product",
    )(part, rtail, etail)
    return grad.T, hvp.T


def solution(mesh):
    placed = (P("dp", None), P("dp"), P("dp"), P("dp", "cls"), P("dp", "cls"))
    body = paired if mesh.shape["dp"] == 2 and mesh.shape["cls"] == 16 else local
    return jax.shard_map(
        body,
        mesh=mesh,
        in_specs=placed,
        out_specs=(P("dp", "cls"), P("dp", "cls")),
        check_vma=False,
    )
```

```python
import functools

import jax
import jax.numpy as jnp
from jax import lax
from jax.experimental import pallas as pl
from jax.experimental.pallas import tpu as pltpu
from jax.sharding import PartitionSpec as P

D = 4096
FOLDS = 5


def local(embeddings, fold_ids, labels, weights, direction):
    row_count = embeddings.shape[0]
    columns = weights.shape[1]
    per_class = columns // FOLDS
    logits = jnp.dot(
        embeddings,
        lax.all_gather(weights, "dp", axis=0, tiled=True),
        preferred_element_type=jnp.float32,
    )
    tangent = jnp.dot(
        embeddings,
        lax.all_gather(direction, "dp", axis=0, tiled=True),
        preferred_element_type=jnp.float32,
    )
    logits = logits.reshape(row_count, per_class, FOLDS)
    tangent = tangent.reshape(row_count, per_class, FOLDS)
    local_high = jnp.max(logits, axis=1)
    highest = lax.pmax(local_high, "cls")
    scaled = jnp.exp(logits - highest[:, None, :])
    summed, moment = lax.psum((jnp.sum(scaled, axis=1), jnp.sum(scaled * tangent, axis=1)), "cls")
    probability = scaled / summed[:, None, :]
    mean_tangent = moment / summed
    class_ids = lax.axis_index("cls") * per_class + jnp.arange(per_class, dtype=jnp.int32)
    onehot = (labels[:, None] == class_ids[None, :]).astype(jnp.float32)[:, :, None]
    training = (fold_ids[:, None] != jnp.arange(FOLDS, dtype=jnp.int32)[None, :]).astype(
        jnp.float32
    )[:, None, :]
    residual_rows = (
        (training * (probability - onehot)).reshape(row_count, columns).astype(jnp.bfloat16)
    )
    curvature = (
        (training * probability * (tangent - mean_tangent[:, None, :]))
        .reshape(row_count, columns)
        .astype(jnp.bfloat16)
    )
    contract = (((0,), (0,)), ((), ()))
    share = D // lax.axis_size("dp")
    full_grad, full_hvp = lax.psum(
        (
            lax.dot_general(
                embeddings, residual_rows, contract, preferred_element_type=jnp.float32
            ),
            lax.dot_general(embeddings, curvature, contract, preferred_element_type=jnp.float32),
        ),
        "dp",
    )
    offset = lax.axis_index("dp") * share
    gradient = lax.dynamic_slice_in_dim(full_grad, offset, share, 0)
    hess_vec = lax.dynamic_slice_in_dim(full_hvp, offset, share, 0)
    return (gradient, hess_vec)


MESH = pl.DeviceIdType.MESH
LANES = 128
SLOTS = FOLDS - 1
NT = (((1,), (1,)), ((), ()))


def pack(nat, base, per, fold):
    blocks = [nat[pl.ds(base + f, per, stride=FOLDS), :] for f in range(FOLDS)]
    return [jnp.where(fold > s, blocks[s], blocks[s + 1]) for s in range(SLOTS)]


def unpack(slots, nat, base, per, fold):
    for f in range(FOLDS):
        if f == 0:
            block = slots[0]
        elif f == FOLDS - 1:
            block = slots[SLOTS - 1]
        else:
            block = jnp.where(fold > f, slots[f], slots[f - 1])
        nat[pl.ds(base + f, per, stride=FOLDS), :] = jnp.where(fold == f, 0.0, block)


def merge(parts):
    high = functools.reduce(jnp.maximum, [p[0] for p in parts])
    total, moment = 0.0, 0.0
    for m, s, t in parts:
        w = jnp.exp(m - high)
        total = total + s * w
        moment = moment + t * w
    return high, total, moment


def split_stats(tile):
    return tile[0:4], tile[4:8], tile[8:12]


def exchange(
    e, wt, dt, folds, labels, partout, rtail, etail,
    part, wd, ee, aux, auxp, res_all, nat_own, nat_peer, xsend, xrecv, xtot, so1, si1, so2, si2, rsend, rrecv,
    lsem, asem, hs, hr, ps, pr, s1s, s1r, s2s, s2r, rs, rr,
):
    rows, share = ee.shape[0] // 2, ee.shape[1]
    cols = wt.shape[0]
    per = cols // FOLDS
    packed = SLOTS * per
    eighth = share // 8
    chunks = xsend.shape[0]
    pieces = [(LANES * k, min(LANES, rows - LANES * k)) for k in range(chunks)]

    def halved(k):
        return pieces[k][1] < LANES

    last = chunks - 1
    low = lax.broadcasted_iota(jnp.int32, (1, LANES), 1) < LANES // 2

    d = lax.axis_index("dp")
    cls = lax.axis_index("cls")
    c = cls % 2
    x = (cls // 2) % 2
    z = cls // 4
    q = 2 * x + c
    other = 1 - d
    core = cls + 1 - 2 * c
    xn = cls + 2 - 4 * x
    group = [core, xn, cls + 3 - 2 * c - 4 * x]
    zs = [z + 1 - 2 * (z % 2), z + 2 - 4 * (z // 2), 3 - z]
    zgroup = [4 * zz + q for zz in zs]
    peer = (other, cls)

    loads = [
        pltpu.make_async_copy(wt, wd.at[pl.ds(0, cols)], lsem.at[0]),
        pltpu.make_async_copy(dt, wd.at[pl.ds(cols, cols)], lsem.at[1]),
    ] + [
        pltpu.make_async_copy(
            e.at[pl.ds(at, size), pl.ds(pl.multiple_of(d * share, share), share)],
            ee.at[pl.ds(2 * at, size)],
            lsem.at[2 + t],
        )
        for t, (at, size) in enumerate(pieces)
    ]
    barrier = pltpu.get_barrier_semaphore()
    partners = [peer] + [(d, g) for g in group] + [(d, g) for g in zgroup]
    for partner in partners:
        pl.semaphore_signal(barrier, inc=1, device_id=partner, device_id_type=MESH)
    for load in loads:
        load.start()
    for base, values in ((0, folds), (8, labels)):
        row = values[...].astype(jnp.float32).reshape(1, rows)
        for k, (at, size) in enumerate(pieces):
            part_row = jnp.concatenate([row[:, at : at + size]] * (LANES // size), axis=1)
            aux[k, base : base + 8, :] = jnp.broadcast_to(part_row, (8, LANES))
    pl.semaphore_wait(barrier, len(partners))

    def remote(src, dst, send, recv, to):
        return pltpu.make_async_remote_copy(
            src_ref=src, dst_ref=dst, send_sem=send, recv_sem=recv,
            device_id=to, device_id_type=MESH,
        )

    zz = z % 2
    zn = cls + 4 - 8 * zz
    p = 4 * zz + q

    def piece(index, base=0):
        return pl.ds(pl.multiple_of(base + index * eighth, eighth), eighth)

    px, pz = p + 2 - 4 * x, p + 4 - 8 * zz
    pd = px + 4 - 8 * zz
    pf = (1 - c) * px + c * pz
    to_diag = (1 - c) * zn + c * xn

    acopy = remote(aux, auxp, asem.at[0], asem.at[1], peer)
    hops = []
    for t, (at, size) in enumerate(pieces):
        r = pl.ds(2 * at + size, size)
        routes = [(p, xn), (p, zn), (p, core), (pf, to_diag), (px, core), (pz, core), (pd, core)]
        hop = [
            remote(
                e.at[pl.ds(at, size), piece(p, other * share)], ee.at[r, piece(p)],
                hs.at[0, t], hr.at[0, t], peer,
            )
        ]
        for j, (index, to) in enumerate(routes):
            block = ee.at[r, piece(index)]
            hop.append(remote(block, block, hs.at[j + 1, t], hr.at[j + 1, t], (d, to)))
        hops.append(hop)
    pcopy, rcopy = [], []
    for k in range(chunks):
        r = pl.ds(0, packed if halved(k) else 2 * packed)
        pcopy.append(remote(xsend.at[k, r], xrecv.at[k, r], ps.at[k], pr.at[k], peer))
        rcopy.append(remote(rsend.at[k, r], rrecv.at[k, r], rs.at[k], rr.at[k], peer))
    s1copy = [
        [remote(so1.at[k], si1.at[k, j], s1s.at[k, j], s1r.at[k, j], (d, g)) for j, g in enumerate(group)]
        for k in range(chunks)
    ]
    s2copy = [
        [remote(so2.at[k], si2.at[k, j], s2s.at[k, j], s2r.at[k, j], (d, g)) for j, g in enumerate(zgroup)]
        for k in range(chunks)
    ]

    acopy.start()
    for hop in hops:
        hop[0].start()

    def store(out, k, halves, first):
        if halved(k):
            joined = []
            for x0, x1 in zip(*halves):
                x1 = pltpu.roll(x1, LANES // 2, 1)
                joined.append(jnp.where(low, x0, x1) if first else jnp.where(low, x1, x0))
            halves = [joined]
        for half, blocks in enumerate(halves):
            for s, block in enumerate(blocks):
                out[k, pl.ds(half * packed + s * per, per), :] = block.astype(out.dtype)

    def received(ref, k, half, s, moved):
        if halved(k):
            block = slot(ref, k, 0, s).astype(jnp.float32)
            return pltpu.roll(block, LANES // 2, 1) if half == moved else block
        return slot(ref, k, half, s).astype(jnp.float32)

    def stage_a(t):
        hops[t][0].wait_recv()
        for j in (1, 2, 3):
            hops[t][j].start()

    def stage_b(t):
        hops[t][1].wait_recv()
        hops[t][2].wait_recv()
        for j in (4, 5, 6):
            hops[t][j].start()

    def stage_x(t):
        hops[t][4].wait_recv()
        hops[t][7].start()

    def stage_c(k):
        if k == 0:
            acopy.wait_recv()
            loads[0].wait()
            loads[1].wait()
        loads[2 + k].wait()
        for j in (3, 5, 6, 7):
            hops[k][j].wait_recv()
        at, size = pieces[k]
        both = lax.dot_general(
            wd[...], ee[pl.ds(2 * at, 2 * size), :], NT, preferred_element_type=jnp.float32
        )
        nat_own[...] = both[:, :LANES]
        nat_peer[...] = both[:, -LANES:]
        fold = auxp[k, 0:1, :]
        store(xsend, k, [pack(nat_peer, half * cols, per, fold) for half in range(2)], False)
        pcopy[k].start()
        fold = aux[k, 0:1, :]
        for half in range(2):
            for s, block in enumerate(pack(nat_own, half * cols, per, fold)):
                xtot[k, pl.ds(half * packed + s * per, per), :] = block

    def slot(ref, k, half, s):
        return ref[k, pl.ds(half * packed + s * per, per), :]

    def stage_d(k):
        pcopy[k].wait_recv()
        for s in range(SLOTS):
            logit = slot(xtot, k, 0, s) + received(xrecv, k, 0, s, 0)
            tangent = slot(xtot, k, 1, s) + received(xrecv, k, 1, s, 0)
            xtot[k, pl.ds(s * per, per), :] = logit
            xtot[k, pl.ds(packed + s * per, per), :] = tangent
            high = jnp.max(logit, axis=0, keepdims=True)
            scaled = jnp.exp(logit - high)
            so1[k, s : s + 1, :] = high
            so1[k, 4 + s : 5 + s, :] = jnp.sum(scaled, axis=0, keepdims=True)
            so1[k, 8 + s : 9 + s, :] = jnp.sum(scaled * tangent, axis=0, keepdims=True)
        so1[k, 12:16, :] = jnp.zeros((4, LANES), jnp.float32)
        for copy in s1copy[k]:
            copy.start()

    def merged(own, incoming, k):
        return merge([split_stats(own[k])] + [split_stats(incoming[k, j]) for j in range(3)])

    def stage_e(k):
        for copy in s1copy[k]:
            copy.wait_recv()
        high, total, moment = merged(so1, si1, k)
        so2[k, 0:4, :] = high
        so2[k, 4:8, :] = total
        so2[k, 8:12, :] = moment
        so2[k, 12:16, :] = jnp.zeros((4, LANES), jnp.float32)
        for copy in s2copy[k]:
            copy.start()

    def stage_f(k):
        for copy in s2copy[k]:
            copy.wait_recv()
        high, total, moment = merged(so2, si2, k)
        inverse = 1.0 / total
        mean = moment * inverse
        fold, label = aux[k, 0:1, :], aux[k, 8:9, :]
        classes = lax.broadcasted_iota(jnp.int32, (per, LANES), 0) + cls * per
        onehot = jnp.where(classes.astype(jnp.float32) == label, 1.0, 0.0)
        res, cur = [], []
        for s in range(SLOTS):
            prob = jnp.exp(slot(xtot, k, 0, s) - high[s : s + 1]) * inverse[s : s + 1]
            res.append(prob - onehot)
            cur.append(prob * (slot(xtot, k, 1, s) - mean[s : s + 1]))
        store(rsend, k, (res, cur), True)
        unpack(res, nat_own, 0, per, fold)
        unpack(cur, nat_own, cols, per, fold)
        if k < last:
            res_all[:, pl.ds(2 * LANES * k, LANES)] = nat_own[...].astype(jnp.bfloat16)

    def stage_g(k):
        rcopy[k].wait_recv()
        fold = auxp[k, 0:1, :]
        for half in range(2):
            slots = [received(rrecv, k, half, s, 1) for s in range(SLOTS)]
            unpack(slots, nat_peer, half * cols, per, fold)
        if k == last:
            tile = jnp.where(low, nat_own[...], pltpu.roll(nat_peer[...], LANES // 2, 1))
            rtail[:, LANES:] = tile.astype(jnp.bfloat16)
        elif k == last - 1:
            rtail[:, :LANES] = nat_peer[...].astype(jnp.bfloat16)
        else:
            res_all[:, pl.ds(2 * LANES * k + LANES, LANES)] = nat_peer[...].astype(jnp.bfloat16)

    near = res_all.shape[1]
    keep = pltpu.make_async_copy(ee.at[pl.ds(near, 2 * rows - near)], etail, lsem.at[2 + chunks])
    width = 512
    spans = [pl.ds(i * width, width) for i in range(share // width)]
    saves = [
        pltpu.make_async_copy(part.at[:, span], partout.at[:, span], lsem.at[3 + chunks + i])
        for i, span in enumerate(spans)
    ]

    def own_product(span, at, size):
        return jnp.dot(
            res_all[:, pl.ds(at, size)], ee[pl.ds(at, size), span],
            preferred_element_type=jnp.float32,
        )

    for step in range(chunks + 3):
        for stage, lag in ((stage_a, 0), (stage_b, 1), (stage_x, 2), (stage_c, 3)):
            if 0 <= step - lag < chunks:
                stage(step - lag)
    keep.start()
    half = 2 * LANES
    for step in range(chunks + 2):
        if step <= last:
            stage_d(step)
        if 0 <= step - 1 <= last:
            stage_e(step - 1)
        if 0 <= step - 2 <= last:
            stage_f(step - 2)
            rcopy[step - 2].start()
        if step == last - 1:
            stage_g(0)
            for span in spans:
                part[:, span] = own_product(span, 0, half)

    for k in range(1, last - 1):
        stage_g(k)
    for i, span in enumerate(spans):
        part[:, span] += own_product(span, half, near - half)
        saves[i].start()
    stage_g(last - 1)
    stage_g(last)

    acopy.wait_send()
    for copies in hops + [pcopy, rcopy]:
        for copy in copies:
            copy.wait_send()
    for k in range(chunks):
        for copy in s1copy[k] + s2copy[k]:
            copy.wait_send()
    keep.wait()
    for save in saves:
        save.wait()


def product(part, rtail, etail, grad, hvp):
    cols = grad.shape[0]
    total = part[...] + jnp.dot(rtail[...], etail[...], preferred_element_type=jnp.float32)
    grad[...] = total[:cols]
    hvp[...] = total[cols:]


def paired(embeddings, fold_ids, labels, weights, direction):
    rows = embeddings.shape[0]
    share, cols = weights.shape
    per = cols // FOLDS
    packed = 2 * SLOTS * per
    chunks = -(-rows // LANES)
    f32, bf16 = jnp.float32, jnp.bfloat16
    hbm = pl.BlockSpec(memory_space=pltpu.HBM)
    vmem = pl.BlockSpec(memory_space=pltpu.VMEM)
    dma = pltpu.SemaphoreType.DMA
    part, rtail, etail = pl.pallas_call(
        exchange,
        out_shape=(
            jax.ShapeDtypeStruct((2 * cols, share), f32),
            jax.ShapeDtypeStruct((2 * cols, 2 * LANES), bf16),
            jax.ShapeDtypeStruct((2 * LANES, share), bf16),
        ),
        in_specs=[hbm, hbm, hbm, vmem, vmem],
        out_specs=(hbm, vmem, hbm),
        scratch_shapes=[
            pltpu.VMEM((2 * cols, share), f32),
            pltpu.VMEM((2 * cols, share), bf16),
            pltpu.VMEM((2 * rows, share), bf16),
            pltpu.VMEM((chunks, 16, LANES), f32),
            pltpu.VMEM((chunks, 16, LANES), f32),
            pltpu.VMEM((2 * cols, 2 * rows - 2 * LANES), bf16),
            pltpu.VMEM((2 * cols, LANES), f32),
            pltpu.VMEM((2 * cols, LANES), f32),
            pltpu.VMEM((chunks, packed, LANES), f32),
            pltpu.VMEM((chunks, packed, LANES), f32),
            pltpu.VMEM((chunks, packed, LANES), f32),
            pltpu.VMEM((chunks, 16, LANES), f32),
            pltpu.VMEM((chunks, 3, 16, LANES), f32),
            pltpu.VMEM((chunks, 16, LANES), f32),
            pltpu.VMEM((chunks, 3, 16, LANES), f32),
            pltpu.VMEM((chunks, packed, LANES), bf16),
            pltpu.VMEM((chunks, packed, LANES), bf16),
            dma((3 + chunks + share // 512,)),
            dma((2,)),
        ]
        + [dma((8, chunks))] * 2
        + [dma((chunks,))] * 2
        + [dma((chunks, 3))] * 4
        + [dma((chunks,))] * 2,
        compiler_params=pltpu.CompilerParams(
            collective_id=0, has_side_effects=True, vmem_limit_bytes=60 * 2**20
        ),
        name="exchange",
    )(embeddings, weights.T, direction.T, fold_ids, labels)

    tile = 256
    grad, hvp = pl.pallas_call(
        product,
        out_shape=(jax.ShapeDtypeStruct((cols, share), f32),) * 2,
        grid=(share // tile,),
        in_specs=[
            pl.BlockSpec((2 * cols, tile), lambda i: (0, i)),
            pl.BlockSpec((2 * cols, 2 * LANES), lambda i: (0, 0)),
            pl.BlockSpec((2 * LANES, tile), lambda i: (0, i)),
        ],
        out_specs=(pl.BlockSpec((cols, tile), lambda i: (0, i)),) * 2,
        compiler_params=pltpu.CompilerParams(vmem_limit_bytes=60 * 2**20),
        name="product",
    )(part, rtail, etail)
    return grad.T, hvp.T


def solution(mesh):
    placed = (P("dp", None), P("dp"), P("dp"), P("dp", "cls"), P("dp", "cls"))
    body = paired if mesh.shape["dp"] == 2 and mesh.shape["cls"] == 16 else local
    return jax.shard_map(
        body,
        mesh=mesh,
        in_specs=placed,
        out_specs=(P("dp", "cls"), P("dp", "cls")),
        check_vma=False,
    )
```

```python
import functools

import jax
import jax.numpy as jnp
from jax import lax
from jax.experimental import pallas as pl
from jax.experimental.pallas import tpu as pltpu
from jax.sharding import PartitionSpec as P

D = 4096
FOLDS = 5


def local(embeddings, fold_ids, labels, weights, direction):
    row_count = embeddings.shape[0]
    columns = weights.shape[1]
    per_class = columns // FOLDS
    logits = jnp.dot(
        embeddings,
        lax.all_gather(weights, "dp", axis=0, tiled=True),
        preferred_element_type=jnp.float32,
    )
    tangent = jnp.dot(
        embeddings,
        lax.all_gather(direction, "dp", axis=0, tiled=True),
        preferred_element_type=jnp.float32,
    )
    logits = logits.reshape(row_count, per_class, FOLDS)
    tangent = tangent.reshape(row_count, per_class, FOLDS)
    local_high = jnp.max(logits, axis=1)
    highest = lax.pmax(local_high, "cls")
    scaled = jnp.exp(logits - highest[:, None, :])
    summed, moment = lax.psum((jnp.sum(scaled, axis=1), jnp.sum(scaled * tangent, axis=1)), "cls")
    probability = scaled / summed[:, None, :]
    mean_tangent = moment / summed
    class_ids = lax.axis_index("cls") * per_class + jnp.arange(per_class, dtype=jnp.int32)
    onehot = (labels[:, None] == class_ids[None, :]).astype(jnp.float32)[:, :, None]
    training = (fold_ids[:, None] != jnp.arange(FOLDS, dtype=jnp.int32)[None, :]).astype(
        jnp.float32
    )[:, None, :]
    residual_rows = (
        (training * (probability - onehot)).reshape(row_count, columns).astype(jnp.bfloat16)
    )
    curvature = (
        (training * probability * (tangent - mean_tangent[:, None, :]))
        .reshape(row_count, columns)
        .astype(jnp.bfloat16)
    )
    contract = (((0,), (0,)), ((), ()))
    share = D // lax.axis_size("dp")
    full_grad, full_hvp = lax.psum(
        (
            lax.dot_general(
                embeddings, residual_rows, contract, preferred_element_type=jnp.float32
            ),
            lax.dot_general(embeddings, curvature, contract, preferred_element_type=jnp.float32),
        ),
        "dp",
    )
    offset = lax.axis_index("dp") * share
    gradient = lax.dynamic_slice_in_dim(full_grad, offset, share, 0)
    hess_vec = lax.dynamic_slice_in_dim(full_hvp, offset, share, 0)
    return (gradient, hess_vec)


MESH = pl.DeviceIdType.MESH
LANES = 128
SLOTS = FOLDS - 1
NT = (((1,), (1,)), ((), ()))


def pack(nat, base, per, fold):
    blocks = [nat[pl.ds(base + f, per, stride=FOLDS), :] for f in range(FOLDS)]
    return [jnp.where(fold > s, blocks[s], blocks[s + 1]) for s in range(SLOTS)]


def unpack(slots, nat, base, per, fold):
    for f in range(FOLDS):
        if f == 0:
            block = slots[0]
        elif f == FOLDS - 1:
            block = slots[SLOTS - 1]
        else:
            block = jnp.where(fold > f, slots[f], slots[f - 1])
        nat[pl.ds(base + f, per, stride=FOLDS), :] = jnp.where(fold == f, 0.0, block)


def merge(parts):
    high = functools.reduce(jnp.maximum, [p[0] for p in parts])
    total, moment = 0.0, 0.0
    for m, s, t in parts:
        w = jnp.exp(m - high)
        total = total + s * w
        moment = moment + t * w
    return high, total, moment


def split_stats(tile):
    return tile[0:4], tile[4:8], tile[8:12]


def exchange(
    e, wt, dt, folds, labels, partout, rtail, etail,
    part, wd, ee, aux, auxp, res_all, nat_own, nat_peer, xsend, xrecv, xtot, so1, si1, so2, si2, rsend, rrecv,
    lsem, asem, ys, yr, xs, xr, c1s, c1r, c2s, c2r, ps, pr, s1s, s1r, s2s, s2r, rs, rr,
):
    rows, share = ee.shape[0] // 2, ee.shape[1]
    cols = wt.shape[0]
    per = cols // FOLDS
    packed = SLOTS * per
    quarter = share // 4
    chunks = xsend.shape[0]
    pieces = [(LANES * k, min(LANES, rows - LANES * k)) for k in range(chunks)]

    def halved(k):
        return pieces[k][1] < LANES

    last = chunks - 1
    low = lax.broadcasted_iota(jnp.int32, (1, LANES), 1) < LANES // 2

    d = lax.axis_index("dp")
    cls = lax.axis_index("cls")
    c = cls % 2
    x = (cls // 2) % 2
    z = cls // 4
    q = 2 * x + c
    other = 1 - d
    core = cls + 1 - 2 * c
    xn = cls + 2 - 4 * x
    group = [core, xn, cls + 3 - 2 * c - 4 * x]
    zs = [z + 1 - 2 * (z % 2), z + 2 - 4 * (z // 2), 3 - z]
    zgroup = [4 * zz + q for zz in zs]
    peer = (other, cls)

    loads = [
        pltpu.make_async_copy(wt, wd.at[pl.ds(0, cols)], lsem.at[0]),
        pltpu.make_async_copy(dt, wd.at[pl.ds(cols, cols)], lsem.at[1]),
    ] + [
        pltpu.make_async_copy(
            e.at[pl.ds(at, size), pl.ds(pl.multiple_of(d * share, share), share)],
            ee.at[pl.ds(2 * at, size)],
            lsem.at[2 + t],
        )
        for t, (at, size) in enumerate(pieces)
    ]
    barrier = pltpu.get_barrier_semaphore()
    partners = [peer] + [(d, g) for g in group] + [(d, g) for g in zgroup]
    for partner in partners:
        pl.semaphore_signal(barrier, inc=1, device_id=partner, device_id_type=MESH)
    for load in loads:
        load.start()
    for base, values in ((0, folds), (8, labels)):
        row = values[...].astype(jnp.float32).reshape(1, rows)
        for k, (at, size) in enumerate(pieces):
            part_row = jnp.concatenate([row[:, at : at + size]] * (LANES // size), axis=1)
            aux[k, base : base + 8, :] = jnp.broadcast_to(part_row, (8, LANES))
    pl.semaphore_wait(barrier, len(partners))

    def remote(src, dst, send, recv, to):
        return pltpu.make_async_remote_copy(
            src_ref=src, dst_ref=dst, send_sem=send, recv_sem=recv,
            device_id=to, device_id_type=MESH,
        )

    qa = pl.ds(pl.multiple_of(q * quarter, quarter), quarter)
    qb = pl.ds(pl.multiple_of((q + 2 - 4 * x) * quarter, quarter), quarter)
    qs = pl.ds(pl.multiple_of(other * share + q * quarter, quarter), quarter)

    acopy = remote(aux, auxp, asem.at[0], asem.at[1], peer)
    ycopy, xcopy, c1copy, c2copy = [], [], [], []
    for t, (at, size) in enumerate(pieces):
        r = pl.ds(2 * at + size, size)
        ycopy.append(remote(e.at[pl.ds(at, size), qs], ee.at[r, qa], ys.at[t], yr.at[t], peer))
        xcopy.append(remote(ee.at[r, qa], ee.at[r, qa], xs.at[t], xr.at[t], (d, xn)))
        c1copy.append(remote(ee.at[r, qa], ee.at[r, qa], c1s.at[t], c1r.at[t], (d, core)))
        c2copy.append(remote(ee.at[r, qb], ee.at[r, qb], c2s.at[t], c2r.at[t], (d, core)))
    pcopy, rcopy = [], []
    for k in range(chunks):
        r = pl.ds(0, packed if halved(k) else 2 * packed)
        pcopy.append(remote(xsend.at[k, r], xrecv.at[k, r], ps.at[k], pr.at[k], peer))
        rcopy.append(remote(rsend.at[k, r], rrecv.at[k, r], rs.at[k], rr.at[k], peer))
    s1copy = [
        [remote(so1.at[k], si1.at[k, j], s1s.at[k, j], s1r.at[k, j], (d, g)) for j, g in enumerate(group)]
        for k in range(chunks)
    ]
    s2copy = [
        [remote(so2.at[k], si2.at[k, j], s2s.at[k, j], s2r.at[k, j], (d, g)) for j, g in enumerate(zgroup)]
        for k in range(chunks)
    ]

    acopy.start()
    for copy in ycopy:
        copy.start()

    def store(out, k, halves, first):
        if halved(k):
            joined = []
            for x0, x1 in zip(*halves):
                x1 = pltpu.roll(x1, LANES // 2, 1)
                joined.append(jnp.where(low, x0, x1) if first else jnp.where(low, x1, x0))
            halves = [joined]
        for half, blocks in enumerate(halves):
            for s, block in enumerate(blocks):
                out[k, pl.ds(half * packed + s * per, per), :] = block.astype(out.dtype)

    def received(ref, k, half, s, moved):
        if halved(k):
            block = slot(ref, k, 0, s).astype(jnp.float32)
            return pltpu.roll(block, LANES // 2, 1) if half == moved else block
        return slot(ref, k, half, s).astype(jnp.float32)

    def stage_a(t):
        ycopy[t].wait_recv()
        xcopy[t].start()
        c1copy[t].start()

    def stage_b(t):
        xcopy[t].wait_recv()
        c2copy[t].start()

    def stage_c(k):
        if k == 0:
            acopy.wait_recv()
            loads[0].wait()
            loads[1].wait()
        loads[2 + k].wait()
        c1copy[k].wait_recv()
        c2copy[k].wait_recv()
        at, size = pieces[k]
        both = lax.dot_general(
            wd[...], ee[pl.ds(2 * at, 2 * size), :], NT, preferred_element_type=jnp.float32
        )
        nat_own[...] = both[:, :LANES]
        nat_peer[...] = both[:, -LANES:]
        fold = auxp[k, 0:1, :]
        store(xsend, k, [pack(nat_peer, half * cols, per, fold) for half in range(2)], False)
        pcopy[k].start()
        fold = aux[k, 0:1, :]
        for half in range(2):
            for s, block in enumerate(pack(nat_own, half * cols, per, fold)):
                xtot[k, pl.ds(half * packed + s * per, per), :] = block

    def slot(ref, k, half, s):
        return ref[k, pl.ds(half * packed + s * per, per), :]

    def stage_d(k):
        pcopy[k].wait_recv()
        for s in range(SLOTS):
            logit = slot(xtot, k, 0, s) + received(xrecv, k, 0, s, 0)
            tangent = slot(xtot, k, 1, s) + received(xrecv, k, 1, s, 0)
            xtot[k, pl.ds(s * per, per), :] = logit
            xtot[k, pl.ds(packed + s * per, per), :] = tangent
            high = jnp.max(logit, axis=0, keepdims=True)
            scaled = jnp.exp(logit - high)
            so1[k, s : s + 1, :] = high
            so1[k, 4 + s : 5 + s, :] = jnp.sum(scaled, axis=0, keepdims=True)
            so1[k, 8 + s : 9 + s, :] = jnp.sum(scaled * tangent, axis=0, keepdims=True)
        so1[k, 12:16, :] = jnp.zeros((4, LANES), jnp.float32)
        for copy in s1copy[k]:
            copy.start()

    def merged(own, incoming, k):
        return merge([split_stats(own[k])] + [split_stats(incoming[k, j]) for j in range(3)])

    def stage_e(k):
        for copy in s1copy[k]:
            copy.wait_recv()
        high, total, moment = merged(so1, si1, k)
        so2[k, 0:4, :] = high
        so2[k, 4:8, :] = total
        so2[k, 8:12, :] = moment
        so2[k, 12:16, :] = jnp.zeros((4, LANES), jnp.float32)
        for copy in s2copy[k]:
            copy.start()

    def stage_f(k):
        for copy in s2copy[k]:
            copy.wait_recv()
        high, total, moment = merged(so2, si2, k)
        inverse = 1.0 / total
        mean = moment * inverse
        fold, label = aux[k, 0:1, :], aux[k, 8:9, :]
        classes = lax.broadcasted_iota(jnp.int32, (per, LANES), 0) + cls * per
        onehot = jnp.where(classes.astype(jnp.float32) == label, 1.0, 0.0)
        res, cur = [], []
        for s in range(SLOTS):
            prob = jnp.exp(slot(xtot, k, 0, s) - high[s : s + 1]) * inverse[s : s + 1]
            res.append(prob - onehot)
            cur.append(prob * (slot(xtot, k, 1, s) - mean[s : s + 1]))
        store(rsend, k, (res, cur), True)
        unpack(res, nat_own, 0, per, fold)
        unpack(cur, nat_own, cols, per, fold)
        if k < last:
            res_all[:, pl.ds(2 * LANES * k, LANES)] = nat_own[...].astype(jnp.bfloat16)

    def stage_g(k):
        rcopy[k].wait_recv()
        fold = auxp[k, 0:1, :]
        for half in range(2):
            slots = [received(rrecv, k, half, s, 1) for s in range(SLOTS)]
            unpack(slots, nat_peer, half * cols, per, fold)
        if k == last:
            tile = jnp.where(low, nat_own[...], pltpu.roll(nat_peer[...], LANES // 2, 1))
            rtail[:, LANES:] = tile.astype(jnp.bfloat16)
        elif k == last - 1:
            rtail[:, :LANES] = nat_peer[...].astype(jnp.bfloat16)
        else:
            res_all[:, pl.ds(2 * LANES * k + LANES, LANES)] = nat_peer[...].astype(jnp.bfloat16)

    near = res_all.shape[1]
    keep = pltpu.make_async_copy(ee.at[pl.ds(near, 2 * rows - near)], etail, lsem.at[2 + chunks])
    width = 512
    spans = [pl.ds(i * width, width) for i in range(share // width)]
    saves = [
        pltpu.make_async_copy(part.at[:, span], partout.at[:, span], lsem.at[3 + chunks + i])
        for i, span in enumerate(spans)
    ]

    def own_product(span, at, size):
        return jnp.dot(
            res_all[:, pl.ds(at, size)], ee[pl.ds(at, size), span],
            preferred_element_type=jnp.float32,
        )

    for step in range(chunks + 2):
        for stage, lag in ((stage_a, 0), (stage_b, 1), (stage_c, 2)):
            if 0 <= step - lag < chunks:
                stage(step - lag)
    keep.start()
    for step in range(chunks + 2):
        if step <= last:
            stage_d(step)
        if step == last:
            for copy in rcopy[: last - 2]:
                copy.start()
        if 0 <= step - 1 <= last:
            stage_e(step - 1)
        if 0 <= step - 2 <= last:
            stage_f(step - 2)
            if step - 2 >= last - 2:
                rcopy[step - 2].start()

    stage_g(0)
    stage_g(1)
    half = 4 * LANES
    for span in spans:
        part[:, span] = own_product(span, 0, half)
    for k in range(2, last - 1):
        stage_g(k)
    for i, span in enumerate(spans):
        part[:, span] += own_product(span, half, near - half)
        saves[i].start()
    stage_g(last - 1)
    stage_g(last)

    acopy.wait_send()
    for copies in (ycopy, xcopy, c1copy, c2copy, pcopy, rcopy):
        for copy in copies:
            copy.wait_send()
    for k in range(chunks):
        for copy in s1copy[k] + s2copy[k]:
            copy.wait_send()
    keep.wait()
    for save in saves:
        save.wait()


def product(part, rtail, etail, grad, hvp):
    for half, out in enumerate((grad, hvp)):
        out[...] = part[half] + jnp.dot(
            rtail[half], etail[...], preferred_element_type=jnp.float32
        )


def paired(embeddings, fold_ids, labels, weights, direction):
    rows = embeddings.shape[0]
    share, cols = weights.shape
    per = cols // FOLDS
    packed = 2 * SLOTS * per
    chunks = -(-rows // LANES)
    f32, bf16 = jnp.float32, jnp.bfloat16
    hbm = pl.BlockSpec(memory_space=pltpu.HBM)
    vmem = pl.BlockSpec(memory_space=pltpu.VMEM)
    dma = pltpu.SemaphoreType.DMA
    part, rtail, etail = pl.pallas_call(
        exchange,
        out_shape=(
            jax.ShapeDtypeStruct((2 * cols, share), f32),
            jax.ShapeDtypeStruct((2 * cols, 2 * LANES), bf16),
            jax.ShapeDtypeStruct((2 * LANES, share), bf16),
        ),
        in_specs=[hbm, hbm, hbm, vmem, vmem],
        out_specs=(hbm, vmem, hbm),
        scratch_shapes=[
            pltpu.VMEM((2 * cols, share), f32),
            pltpu.VMEM((2 * cols, share), bf16),
            pltpu.VMEM((2 * rows, share), bf16),
            pltpu.VMEM((chunks, 16, LANES), f32),
            pltpu.VMEM((chunks, 16, LANES), f32),
            pltpu.VMEM((2 * cols, 2 * rows - 2 * LANES), bf16),
            pltpu.VMEM((2 * cols, LANES), f32),
            pltpu.VMEM((2 * cols, LANES), f32),
            pltpu.VMEM((chunks, packed, LANES), f32),
            pltpu.VMEM((chunks, packed, LANES), f32),
            pltpu.VMEM((chunks, packed, LANES), f32),
            pltpu.VMEM((chunks, 16, LANES), f32),
            pltpu.VMEM((chunks, 3, 16, LANES), f32),
            pltpu.VMEM((chunks, 16, LANES), f32),
            pltpu.VMEM((chunks, 3, 16, LANES), f32),
            pltpu.VMEM((chunks, packed, LANES), bf16),
            pltpu.VMEM((chunks, packed, LANES), bf16),
            dma((3 + chunks + share // 512,)),
            dma((2,)),
        ]
        + [dma((chunks,))] * 10
        + [dma((chunks, 3))] * 4
        + [dma((chunks,))] * 2,
        compiler_params=pltpu.CompilerParams(
            collective_id=0, has_side_effects=True, vmem_limit_bytes=60 * 2**20
        ),
        name="exchange",
    )(embeddings, weights.T, direction.T, fold_ids, labels)

    block = cols // 4
    grad, hvp = pl.pallas_call(
        product,
        out_shape=(jax.ShapeDtypeStruct((cols, share), f32),) * 2,
        grid=(cols // block,),
        in_specs=[
            pl.BlockSpec((2, block, share), lambda i: (0, i, 0)),
            pl.BlockSpec((2, block, 2 * LANES), lambda i: (0, i, 0)),
            pl.BlockSpec((2 * LANES, share), lambda i: (0, 0)),
        ],
        out_specs=(pl.BlockSpec((block, share), lambda i: (i, 0)),) * 2,
        compiler_params=pltpu.CompilerParams(vmem_limit_bytes=60 * 2**20),
        name="product",
    )(part.reshape(2, cols, share), rtail.reshape(2, cols, 2 * LANES), etail)
    return grad.T, hvp.T


def solution(mesh):
    placed = (P("dp", None), P("dp"), P("dp"), P("dp", "cls"), P("dp", "cls"))
    body = paired if mesh.shape["dp"] == 2 and mesh.shape["cls"] == 16 else local
    return jax.shard_map(
        body,
        mesh=mesh,
        in_specs=placed,
        out_specs=(P("dp", "cls"), P("dp", "cls")),
        check_vma=False,
    )
```
